256 devices in a mesh: frame: 16 (over x, z_lo, core), row: 16 (over y, z_hi).
Axes of the slice: x: 4, y: 4, z: 8 (z_hi: 4, z_lo: 2; z = z_hi * 2 + z_lo), core: 2. Of those that a mesh axis runs over, the one named last changes fastest.
Arguments:
- query: bfloat16 [16, 32, 80, 1536], P('frame', 'row'), may hold values from -6 to 6
- key: bfloat16 [16, 32, 80, 1536], P('frame', 'row'), may hold values from -6 to 6
- value: bfloat16 [16, 32, 80, 1536], P('frame', 'row'), may hold values from -6 to 6
- key_frames: int32 [16, 4], replicated, may hold values from 0 to 15, as said below
- reach: int32 [16, 4], replicated, may hold values from 0 to 1
- used: int32 [16], replicated, may hold values from 1 to 4
Outputs:
- attended: bfloat16 [16, 32, 80, 1536], P('frame', 'row')
The draws below stay inside these ranges and needn't reach their ends.
Inputs may be any that keep to these rules, and one draw needn't show every extreme that they name: `key_frames`: entry 0 of row f is f itself; every entry j >= 1 of row f is (f + s * 2**p) modulo 16 with s = 1 or s = -1 and 0 <= p <= 2; entries may repeat.
All inputs are finite; a program needn't handle non-finite values.
Results may differ from the reference program's by a relative error of at most 0.0055.
Values may be sent and summed in bfloat16 or wider, within the bound.
A program may use at most 256 MiB of HBM per device.

```python
import jax
import jax.numpy as jnp
from jax import lax

HEADS = 12
HEAD_DIM = 128
COLS = 80
SLOTS = 4
FRAME_DEV = 1
FRAMES = 16
ROWS = 32
FEATURES = 1536


def draw_query(key, part):
    shape = (FRAMES, ROWS, COLS, HEADS * HEAD_DIM)
    key = jax.random.fold_in(key, 5)
    base = jnp.clip(jax.random.normal(key, shape, jnp.float32), -6.0, 6.0)
    return base.astype(jnp.bfloat16)


def draw_key(key, part):
    shape = (FRAMES, ROWS, COLS, HEADS * HEAD_DIM)
    key = jax.random.fold_in(key, 6)
    base = jnp.clip(jax.random.normal(key, shape, jnp.float32), -6.0, 6.0)
    return base.astype(jnp.bfloat16)


def draw_key_frames(key, part):
    key = jax.random.fold_in(key, 7)
    sign_key, power_key = jax.random.split(key)
    signs = jax.random.randint(sign_key, (FRAMES, SLOTS - 1), 0, 2, dtype=jnp.int32) * 2 - 1
    powers = jax.random.randint(power_key, (FRAMES, SLOTS - 1), 0, SLOTS - 1, dtype=jnp.int32)
    strides = FRAME_DEV * jnp.left_shift(jnp.ones_like(powers), powers)
    frame_ids = jnp.arange(FRAMES, dtype=jnp.int32)[:, None]
    others = (frame_ids + signs * strides) % FRAMES
    return jnp.concatenate([frame_ids, others], axis=1).astype(jnp.int32)


def draw_reach(key, part):
    key = jax.random.fold_in(key, 8)
    spans = jax.random.randint(key, (FRAMES, SLOTS), 0, 2, dtype=jnp.int32)
    return spans.at[:, 0].set(1)


def draw_used(key, part):
    key = jax.random.fold_in(key, 9)
    first_key, second_key = jax.random.split(key)
    counts = jax.random.randint(first_key, (FRAMES,), 1, SLOTS + 1, dtype=jnp.int32)
    forced = jax.random.randint(second_key, (), 0, FRAMES, dtype=jnp.int32)
    return jnp.where(jnp.arange(FRAMES, dtype=jnp.int32) == forced, SLOTS, counts).astype(jnp.int32)


def shard_levels(rng, dims, shards, smallest, largest):
    factor_of = 1.0
    for dim, parts in shards:
        draws = jax.random.uniform(jax.random.fold_in(jax.random.fold_in(rng, 6), dim), (parts,), jnp.float32, smallest / len(shards), largest / len(shards))
        factor_of = factor_of * jnp.repeat(jnp.exp(draws), dims[dim] // parts).reshape((-1,) + (1,) * (len(dims) - 1 - dim))
    return factor_of


def noise(rng, dims, deviation, most, cuts=(), held_as=jnp.bfloat16):
    gain = shard_levels(rng, dims, cuts, -0.22, 0.18) if cuts else 1.0
    values = jax.random.normal(rng, dims, jnp.float32) * deviation * gain
    return jnp.minimum(jnp.maximum(values, -most), most).astype(held_as)


def setup_inputs(seed: int = 0) -> dict:
    splits = jax.random.split(jax.random.key(seed), 7)
    query = draw_query(jax.random.fold_in(splits[6], 71), 0)
    key = draw_key(jax.random.fold_in(splits[6], 71), 0)
    value = noise(splits[2], (FRAMES, ROWS, COLS, FEATURES), 1.0, 6.0, ((0, 16), (1, 16)))
    key_frames = draw_key_frames(jax.random.fold_in(splits[6], 71), 0)
    reach = draw_reach(jax.random.fold_in(splits[6], 71), 0)
    used = draw_used(jax.random.fold_in(splits[6], 71), 0)
    return dict(query=query, key=key, value=value, key_frames=key_frames, reach=reach, used=used)


def reference(query, key, value, key_frames, reach, used):
    frame_total, row_total, columns, features = query.shape
    head_count = features // HEAD_DIM
    slot_count = key_frames.shape[1]
    key_padded = jnp.pad(key, ((0, 0), (1, 1), (0, 0), (0, 0)))
    value_padded = jnp.pad(value, ((0, 0), (1, 1), (0, 0), (0, 0)))
    offsets = jnp.arange(3, dtype=jnp.int32) - 1
    zero_index = jnp.zeros((), jnp.int32)
    slot_ids = jnp.arange(slot_count, dtype=jnp.int32)

    def fetch(padded, target, row_pick):
        start = (target.astype(jnp.int32), row_pick.astype(jnp.int32), zero_index, zero_index)
        return lax.dynamic_slice(padded, start, (1, 3, columns, features))[0]

    def one_row(position):
        frame_pick = (position // row_total).astype(jnp.int32)
        row_pick = (position % row_total).astype(jnp.int32)
        query_row = lax.dynamic_slice(query, (frame_pick, row_pick, zero_index, zero_index), (1, 1, columns, features))
        query_row = query_row.reshape(columns, head_count, HEAD_DIM).astype(jnp.float32)
        targets = lax.dynamic_index_in_dim(key_frames, frame_pick, 0, False)
        spans = lax.dynamic_index_in_dim(reach, frame_pick, 0, False)
        live_count = lax.dynamic_index_in_dim(used, frame_pick, 0, False)
        live = slot_ids < live_count
        same = (targets[:, None] == targets[None, :]) & live[None, :]
        widest = jnp.max(jnp.where(same, spans[None, :], -1), axis=1)
        earlier = jnp.any(same & (slot_ids[None, :] < slot_ids[:, None]), axis=1)
        first = live & jnp.logical_not(earlier)
        keys_near = jax.vmap(lambda target: fetch(key_padded, target, row_pick))(targets)
        keys_near = keys_near.reshape(slot_count * 3 * columns, head_count, HEAD_DIM).astype(jnp.float32)
        values_near = jax.vmap(lambda target: fetch(value_padded, target, row_pick))(targets)
        values_near = values_near.reshape(slot_count * 3 * columns, head_count, HEAD_DIM).astype(jnp.float32)
        rows_seen = row_pick + offsets
        allowed = first[:, None]
        allowed = allowed & (jnp.abs(offsets)[None, :] <= widest[:, None])
        allowed = allowed & ((rows_seen >= 0) & (rows_seen < row_total))[None, :]
        allowed = jnp.broadcast_to(allowed[:, :, None], (slot_count, 3, columns)).reshape(slot_count * 3 * columns)
        scores = jnp.einsum("chd,khd->hck", query_row, keys_near, precision=lax.Precision.HIGHEST) * (HEAD_DIM ** -0.5)
        scores = jnp.where(allowed[None, None, :], scores, -jnp.inf)
        peak = jnp.max(scores, axis=2, keepdims=True)
        weights = jnp.exp(scores - peak)
        totals = jnp.sum(weights, axis=2)
        weights_low = weights.astype(jnp.bfloat16).astype(jnp.float32)
        mixed = jnp.einsum("hck,khd->chd", weights_low, values_near, precision=lax.Precision.HIGHEST)
        mixed = mixed / jnp.transpose(totals)[:, :, None]
        return mixed.reshape(columns, features).astype(jnp.bfloat16)

    rows_out = lax.map(one_row, jnp.arange(frame_total * row_total, dtype=jnp.int32))
    return rows_out.reshape(query.shape)
```

```python
import functools

import jax
import jax.numpy as jnp
from jax import lax
from jax.experimental import pallas as pl
from jax.experimental.pallas import tpu as pltpu
from jax.sharding import PartitionSpec as P


HEAD_DIM = 128
MESH = pl.DeviceIdType.MESH
NEG = -1e30


def body(frames, pairs, cols, slots, kf_ref, reach_ref, used_ref, q_ref, k_ref, v_ref, o_ref,
         buf_a, buf_b, out_a, out_b, main_send, main_recv, rim_send, rim_recv, out_send, out_recv):
    me = lax.axis_index("frame")
    pair = lax.axis_index("row")
    core = lax.rem(me, 2)
    half = lax.rem(me // 2, 2)
    bufs, outs = (buf_a, buf_b), (out_a, out_b)
    keys = 3 * cols
    two = 2 * cols
    v_at, q_at = keys, 2 * keys
    has_rim = jnp.logical_or(
        jnp.logical_and(half == 1, pair < pairs - 1), jnp.logical_and(half == 0, pair > 0)
    )
    rim_pair = jnp.where(half == 1, pair + 1, pair - 1)
    rim_frame = 4 * (me // 4) + 2 * (1 - half) + core
    rim_row = pl.multiple_of(half * cols, cols)

    def head_of(device, slot):
        return 3 * (device // 4) + (2 * lax.rem(device, 2) if slot == 0 else 1)

    barrier = pltpu.get_barrier_semaphore()

    @pl.loop(1, frames)
    def _(d):
        pl.semaphore_signal(barrier, inc=1, device_id=(lax.rem(me + d, frames), pair), device_id_type=MESH)

    @pl.when(has_rim)
    def _():
        pl.semaphore_signal(barrier, inc=1, device_id=(rim_frame, rim_pair), device_id_type=MESH)
        pl.semaphore_wait(barrier, frames)

    @pl.when(jnp.logical_not(has_rim))
    def _():
        pl.semaphore_wait(barrier, frames - 1)

    def pieces(device, slot):
        buf = bufs[slot]
        col = pl.multiple_of(head_of(device, slot) * HEAD_DIM, HEAD_DIM)
        q_row = pl.multiple_of(lax.rem(device // 2, 2) * cols, cols)
        at = pl.ds(col, HEAD_DIM)
        return (
            (k_ref.at[:, at], buf.at[me, pl.ds(0, two)]),
            (v_ref.at[:, at], buf.at[me, pl.ds(v_at, two)]),
            (q_ref.at[pl.ds(q_row, cols), at], buf.at[me, pl.ds(q_at, cols)]),
        )

    def send_main(device, slot):
        for src, dst in pieces(device, slot):
            pltpu.make_async_remote_copy(
                src_ref=src, dst_ref=dst, send_sem=main_send.at[slot, device], recv_sem=main_recv.at[slot, me],
                device_id=(device, pair), device_id_type=MESH,
            ).start()

    def keep_main(slot):
        for src, dst in pieces(me, slot):
            pltpu.make_async_copy(src, dst, main_recv.at[slot, me]).start()

    def wait_rows(ref, frame, rows, sem):
        view = ref.at[frame, pl.ds(0, rows)]
        pltpu.make_async_copy(view, view, sem).wait()

    keep_main(0)

    @pl.loop(1, frames)
    def _(d):
        send_main(lax.rem(me + d, frames), 0)

    @pl.when(core == 0)
    def _():
        keep_main(1)

    @pl.loop(1, frames)
    def _(d):
        device = lax.rem(me + d, frames)

        @pl.when(lax.rem(device, 2) == 0)
        def _():
            send_main(device, 1)

    def pass_rim(frame, slot):
        buf = bufs[slot]
        wait_rows(buf, frame, 2 * two + cols, main_recv.at[slot, frame])

        @pl.when(has_rim)
        def _():
            for base in (0, v_at):
                pltpu.make_async_remote_copy(
                    src_ref=buf.at[frame, pl.ds(pl.multiple_of(base + rim_row, cols), cols)],
                    dst_ref=buf.at[frame, pl.ds(base + two, cols)],
                    send_sem=rim_send.at[slot, frame], recv_sem=rim_recv.at[slot, frame],
                    device_id=(rim_frame, rim_pair), device_id_type=MESH,
                ).start()

    def clear_rim(slot):
        @pl.when(jnp.logical_not(has_rim))
        def _():
            @pl.loop(0, frames)
            def _(frame):
                for base in (0, v_at):
                    bufs[slot][frame, pl.ds(base + two, cols), :] = jnp.zeros((cols, HEAD_DIM), jnp.bfloat16)

    def wait_rim(slot):
        @pl.when(has_rim)
        def _():
            @pl.loop(0, frames)
            def _(frame):
                wait_rows(bufs[slot], frame, two, rim_recv.at[slot, frame])

    key_row = lax.broadcasted_iota(jnp.int32, (1, keys), 1) // cols
    distance = jnp.where(key_row == half, 0, 1)
    distance = jnp.where(jnp.logical_and(key_row == 2, jnp.logical_not(has_rim)), 9, distance)
    factor = HEAD_DIM ** -0.5 * 1.4426950408889634

    def attend(frame, slot):
        buf = bufs[slot]
        q = buf[frame, pl.ds(q_at, cols), :]
        targets = [kf_ref[j, frame] for j in range(slots)]
        spans = [jnp.where(j < used_ref[frame], reach_ref[j, frame], -1) for j in range(slots)]
        scores = []
        for j in range(slots):
            spread = spans[j]
            for i in range(slots):
                if i != j:
                    same = targets[i] == targets[j]
                    spread = jnp.maximum(spread, jnp.where(same, spans[i], -1))
            for i in range(j):
                spread = jnp.where(jnp.logical_and(targets[i] == targets[j], spans[i] >= 0), -1, spread)
            spread = jnp.where(spans[j] >= 0, spread, -1)
            s = lax.dot_general(
                q, buf[targets[j], pl.ds(0, keys), :], (((1,), (1,)), ((), ())), preferred_element_type=jnp.float32
            )
            scores.append(s * factor + jnp.where(distance <= spread, 0.0, NEG))
        peak = functools.reduce(jnp.maximum, scores)
        peak = jnp.max(peak, axis=1, keepdims=True)
        weights = [jnp.exp2(s - peak) for s in scores]
        total = jnp.sum(functools.reduce(jnp.add, weights), axis=1, keepdims=True)
        mixed = None
        for j in range(slots):
            part = lax.dot_general(
                weights[j].astype(jnp.bfloat16), buf[targets[j], pl.ds(v_at, keys), :],
                (((1,), (0,)), ((), ())), preferred_element_type=jnp.float32,
            )
            mixed = part if mixed is None else mixed + part
        outs[slot][frame] = (mixed / total).astype(jnp.bfloat16)

    def out_view(slot):
        col = pl.multiple_of(head_of(me, slot) * HEAD_DIM, HEAD_DIM)
        return o_ref.at[pl.ds(pl.multiple_of(half * cols, cols), cols), pl.ds(col, HEAD_DIM)]

    def send_out(frame, slot):
        @pl.when(frame == me)
        def _():
            pltpu.make_async_copy(outs[slot].at[frame], out_view(slot), out_recv.at[slot, me]).start()

        @pl.when(frame != me)
        def _():
            pltpu.make_async_remote_copy(
                src_ref=outs[slot].at[frame], dst_ref=out_view(slot),
                send_sem=out_send.at[slot, frame], recv_sem=out_recv.at[slot, me],
                device_id=(frame, pair), device_id_type=MESH,
            ).start()

    clear_rim(0)

    @pl.loop(0, frames)
    def _(d):
        pass_rim(lax.rem(me + frames - d, frames), 0)

    wait_rim(0)

    @pl.loop(0, frames)
    def _(d):
        frame = lax.rem(me + d, frames)
        attend(frame, 0)
        send_out(frame, 0)

        @pl.when(core == 0)
        def _():
            pass_rim(lax.rem(me + frames - d, frames), 1)

    @pl.when(core == 0)
    def _():
        clear_rim(1)
        wait_rim(1)

        @pl.loop(0, frames)
        def _(d):
            frame = lax.rem(me + d, frames)
            attend(frame, 1)
            send_out(frame, 1)

    @pl.loop(0, frames)
    def _(device):
        even = lax.rem(device, 2) == 0
        other = device != me

        @pl.when(other)
        def _():
            wait_rows(buf_a, 0, 2 * two + cols, main_send.at[0, device])
            wait_rows(out_a, 0, cols, out_send.at[0, device])

            @pl.when(even)
            def _():
                wait_rows(buf_b, 0, 2 * two + cols, main_send.at[1, device])

            @pl.when(core == 0)
            def _():
                wait_rows(out_b, 0, cols, out_send.at[1, device])

        @pl.when(has_rim)
        def _():
            wait_rows(buf_a, 0, two, rim_send.at[0, device])

            @pl.when(core == 0)
            def _():
                wait_rows(buf_b, 0, two, rim_send.at[1, device])

        wait_rows(out_a, 0, cols, out_recv.at[0, device])

        @pl.when(even)
        def _():
            wait_rows(out_b, 0, cols, out_recv.at[1, device])


def local(query, key, value, key_frames, reach, used):
    _, rows, cols, features = query.shape
    frames, pairs = lax.axis_size("frame"), lax.axis_size("row")
    slots = key_frames.shape[1]
    flat = (rows * cols, features)
    block = (frames, 7 * cols, HEAD_DIM)
    out_block = (frames, cols, HEAD_DIM)
    smem = pl.BlockSpec(memory_space=pltpu.SMEM)
    hbm = pl.BlockSpec(memory_space=pl.ANY)
    out = pl.pallas_call(
        functools.partial(body, frames, pairs, cols, slots),
        out_shape=jax.ShapeDtypeStruct(flat, jnp.bfloat16),
        in_specs=[smem, smem, smem, hbm, hbm, hbm],
        out_specs=hbm,
        scratch_shapes=[
            pltpu.VMEM(block, jnp.bfloat16),
            pltpu.VMEM(block, jnp.bfloat16),
            pltpu.VMEM(out_block, jnp.bfloat16),
            pltpu.VMEM(out_block, jnp.bfloat16),
        ] + [pltpu.SemaphoreType.DMA((2, frames))] * 6,
        compiler_params=pltpu.CompilerParams(
            collective_id=0, has_side_effects=True, vmem_limit_bytes=40 * 1024 * 1024
        ),
        cost_estimate=pl.CostEstimate(flops=2 * 10**9, bytes_accessed=10**7, transcendentals=10**7),
    )(key_frames.T, reach.T, used, query.reshape(flat), key.reshape(flat), value.reshape(flat))
    return out.reshape(query.shape)


def solution(mesh):
    return jax.shard_map(
        local,
        mesh=mesh,
        in_specs=(
            P("frame", "row", None, None),
            P("frame", "row", None, None),
            P("frame", "row", None, None),
            P(),
            P(),
            P(),
        ),
        out_specs=P("frame", "row", None, None),
        check_vma=False,
    )
```

```python
import functools

import jax
import jax.numpy as jnp
from jax import lax
from jax.experimental import pallas as pl
from jax.experimental.pallas import tpu as pltpu
from jax.sharding import PartitionSpec as P


HEAD_DIM = 128
MESH = pl.DeviceIdType.MESH
NEG = -1e30


def body(frames, pairs, cols, slots, kf_ref, reach_ref, used_ref, q_ref, k_ref, v_ref, o_ref,
         buf_a, buf_b, out_a, out_b, kv_recv, q_recv, main_send, rim_send, rim_recv, out_send, out_recv):
    me = lax.axis_index("frame")
    pair = lax.axis_index("row")
    core = lax.rem(me, 2)
    half = lax.rem(me // 2, 2)
    bufs, outs = (buf_a, buf_b), (out_a, out_b)
    keys = 3 * cols
    two = 2 * cols
    v_at, q_at = keys, 2 * keys
    has_rim = jnp.logical_or(
        jnp.logical_and(half == 1, pair < pairs - 1), jnp.logical_and(half == 0, pair > 0)
    )
    no_rim = jnp.logical_not(has_rim)
    rim_pair = jnp.where(half == 1, pair + 1, pair - 1)
    rim_frame = 4 * (me // 4) + 2 * (1 - half) + core
    rim_row = pl.multiple_of(half * cols, cols)

    def head_of(device, slot):
        return 3 * (device // 4) + (2 * lax.rem(device, 2) if slot == 0 else 1)

    def chip(step, sign):
        k = step // 2
        distance = k + k // 2 - 2 * (k // 2) * lax.rem(k, 2)
        x = lax.rem(me // 4 + 4 + sign * distance, 4)
        return 4 * x + 2 * lax.rem(half + 1 + step, 2)

    barrier = pltpu.get_barrier_semaphore()

    @pl.loop(1, frames)
    def _(d):
        pl.semaphore_signal(barrier, inc=1, device_id=(lax.rem(me + d, frames), pair), device_id_type=MESH)

    @pl.when(has_rim)
    def _():
        pl.semaphore_signal(barrier, inc=1, device_id=(rim_frame, rim_pair), device_id_type=MESH)

    def kv_pieces(device, slot):
        at = pl.ds(pl.multiple_of(head_of(device, slot) * HEAD_DIM, HEAD_DIM), HEAD_DIM)
        buf = bufs[slot]
        return (
            (k_ref.at[:, at], buf.at[me, pl.ds(0, two)]),
            (v_ref.at[:, at], buf.at[me, pl.ds(v_at, two)]),
        )

    def q_piece(device, slot):
        at = pl.ds(pl.multiple_of(head_of(device, slot) * HEAD_DIM, HEAD_DIM), HEAD_DIM)
        row = pl.multiple_of(lax.rem(device // 2, 2) * cols, cols)
        return q_ref.at[pl.ds(row, cols), at], bufs[slot].at[me, pl.ds(q_at, cols)]

    def keep(slot):
        for src, dst in kv_pieces(me, slot):
            pltpu.make_async_copy(src, dst, kv_recv.at[slot, me]).start()
        src, dst = q_piece(me, slot)
        pltpu.make_async_copy(src, dst, q_recv.at[slot]).start()

    def send(src, dst, slot, recv_sem, device):
        pltpu.make_async_remote_copy(
            src_ref=src, dst_ref=dst, send_sem=main_send.at[slot], recv_sem=recv_sem,
            device_id=(device, pair), device_id_type=MESH,
        ).start()

    def send_kv(device, slot):
        for src, dst in kv_pieces(device, slot):
            send(src, dst, slot, kv_recv.at[slot, me], device)

    def send_q(device, slot):
        src, dst = q_piece(device, slot)
        send(src, dst, slot, q_recv.at[slot], device)

    def settle(view, sem):
        pltpu.make_async_copy(view, view, sem).wait()

    keep(0)

    @pl.when(core == 0)
    def _():
        keep(1)

    @pl.when(has_rim)
    def _():
        pl.semaphore_wait(barrier, frames)

    @pl.when(no_rim)
    def _():
        pl.semaphore_wait(barrier, frames - 1)

    @pl.loop(0, frames // 2)
    def _(step):
        for c in range(2):
            device = chip(step, 1) + c

            @pl.when(device != me)
            def _():
                send_kv(device, 0)
                send_q(device, 0)

    @pl.loop(0, frames // 2)
    def _(step):
        device = chip(step, 1)

        @pl.when(device != me)
        def _():
            send_kv(device, 1)

    @pl.loop(0, frames // 2)
    def _(step):
        device = chip(step, 1)

        @pl.when(device != me)
        def _():
            send_q(device, 1)

    def pass_rim(frame, slot):
        buf = bufs[slot]
        settle(buf.at[frame, pl.ds(0, 2 * two)], kv_recv.at[slot, frame])

        @pl.when(has_rim)
        def _():
            for base in (0, v_at):
                pltpu.make_async_remote_copy(
                    src_ref=buf.at[frame, pl.ds(pl.multiple_of(base + rim_row, cols), cols)],
                    dst_ref=buf.at[frame, pl.ds(base + two, cols)],
                    send_sem=rim_send.at[slot], recv_sem=rim_recv.at[slot],
                    device_id=(rim_frame, rim_pair), device_id_type=MESH,
                ).start()

    def pass_rims(step, slot):
        for c in range(2):
            pass_rim(chip(step, -1) + c, slot)

    def clear_rim(slot):
        @pl.loop(0, frames)
        def _(frame):
            for base in (0, v_at):
                bufs[slot][frame, pl.ds(base + two, cols), :] = jnp.zeros((cols, HEAD_DIM), jnp.bfloat16)

    def wait_rest(slot):
        settle(bufs[slot].at[:, pl.ds(0, cols)], q_recv.at[slot])

        @pl.when(has_rim)
        def _():
            settle(bufs[slot].at[:, pl.ds(0, two)], rim_recv.at[slot])

    key_row = lax.broadcasted_iota(jnp.int32, (1, keys), 1) // cols
    distance = jnp.where(key_row == half, 0, 1)
    distance = jnp.where(jnp.logical_and(key_row == 2, no_rim), 9, distance)
    factor = HEAD_DIM ** -0.5 * 1.4426950408889634

    def spreads(frame):
        targets = [kf_ref[j, frame] for j in range(slots)]
        spans = [jnp.where(j < used_ref[frame], reach_ref[j, frame], -1) for j in range(slots)]
        found = []
        for j in range(slots):
            spread = spans[j]
            for i in range(slots):
                if i != j:
                    spread = jnp.maximum(spread, jnp.where(targets[i] == targets[j], spans[i], -1))
            for i in range(j):
                spread = jnp.where(jnp.logical_and(targets[i] == targets[j], spans[i] >= 0), -1, spread)
            found.append(jnp.where(spans[j] >= 0, spread, -1))
        return targets, found

    def attend(group, slot):
        buf = bufs[slot]
        masks = [spreads(frame) for frame in group]
        scores = [
            [
                lax.dot_general(
                    buf[frame, pl.ds(q_at, cols), :], buf[target, pl.ds(0, keys), :],
                    (((1,), (1,)), ((), ())), preferred_element_type=jnp.float32,
                )
                for target in targets
            ]
            for frame, (targets, _) in zip(group, masks)
        ]
        weights, totals = [], []
        for row, (_, found) in zip(scores, masks):
            row = [s * factor + jnp.where(distance <= spread, 0.0, NEG) for s, spread in zip(row, found)]
            peak = jnp.max(functools.reduce(jnp.maximum, row), axis=1, keepdims=True)
            row = [jnp.exp2(s - peak) for s in row]
            totals.append(jnp.sum(functools.reduce(jnp.add, row), axis=1, keepdims=True))
            weights.append(row)
        mixed = [
            functools.reduce(jnp.add, [
                lax.dot_general(
                    w.astype(jnp.bfloat16), buf[target, pl.ds(v_at, keys), :],
                    (((1,), (0,)), ((), ())), preferred_element_type=jnp.float32,
                )
                for w, target in zip(row, targets)
            ])
            for row, (targets, _) in zip(weights, masks)
        ]
        for frame, value, total in zip(group, mixed, totals):
            outs[slot][frame] = (value / total).astype(jnp.bfloat16)

    out_col = [pl.multiple_of(head_of(me, slot) * HEAD_DIM, HEAD_DIM) for slot in range(2)]
    out_row = pl.multiple_of(half * cols, cols)

    def send_out(frame, slot):
        view = o_ref.at[pl.ds(out_row, cols), pl.ds(out_col[slot], HEAD_DIM)]

        @pl.when(frame == me)
        def _():
            pltpu.make_async_copy(outs[slot].at[frame], view, out_recv.at[slot]).start()

        @pl.when(frame != me)
        def _():
            pltpu.make_async_remote_copy(
                src_ref=outs[slot].at[frame], dst_ref=view, send_sem=out_send.at[slot], recv_sem=out_recv.at[slot],
                device_id=(frame, pair), device_id_type=MESH,
            ).start()

    def work(step, slot):
        group = [lax.rem(me + 4 * step + u, frames) for u in range(4)]
        attend(group, slot)
        for frame in group:
            send_out(frame, slot)

    @pl.when(no_rim)
    def _():
        clear_rim(0)
        clear_rim(1)

    @pl.loop(0, frames // 2)
    def _(step):
        pass_rims(step, 0)

    wait_rest(0)

    @pl.loop(0, frames // 4)
    def _(step):
        work(step, 0)

        @pl.when(core == 0)
        def _():
            for i in range(2):
                pass_rims(2 * step + i, 1)

    @pl.when(core == 0)
    def _():
        wait_rest(1)

        @pl.loop(0, frames // 4)
        def _(step):
            work(step, 1)

    settle(buf_a.at[pl.ds(0, frames - 1), pl.ds(0, 2 * two + cols)], main_send.at[0])
    settle(out_a.at[pl.ds(0, frames - 1)], out_send.at[0])

    @pl.when(has_rim)
    def _():
        settle(buf_a.at[:, pl.ds(0, two)], rim_send.at[0])

    @pl.when(core == 0)
    def _():
        settle(buf_b.at[pl.ds(0, frames // 2 - 1), pl.ds(0, 2 * two + cols)], main_send.at[1])
        settle(out_b.at[pl.ds(0, frames - 1)], out_send.at[1])

        @pl.when(has_rim)
        def _():
            settle(buf_b.at[:, pl.ds(0, two)], rim_send.at[1])

    @pl.when(core == 1)
    def _():
        settle(buf_b.at[pl.ds(0, frames // 2), pl.ds(0, 2 * two + cols)], main_send.at[1])

    settle(out_a, out_recv.at[0])
    settle(out_b.at[pl.ds(0, frames // 2)], out_recv.at[1])


def local(query, key, value, key_frames, reach, used):
    _, rows, cols, features = query.shape
    frames, pairs = lax.axis_size("frame"), lax.axis_size("row")
    slots = key_frames.shape[1]
    flat = (rows * cols, features)
    block = (frames, 7 * cols, HEAD_DIM)
    out_block = (frames, cols, HEAD_DIM)
    smem = pl.BlockSpec(memory_space=pltpu.SMEM)
    hbm = pl.BlockSpec(memory_space=pl.ANY)
    out = pl.pallas_call(
        functools.partial(body, frames, pairs, cols, slots),
        out_shape=jax.ShapeDtypeStruct(flat, jnp.bfloat16),
        in_specs=[smem, smem, smem, hbm, hbm, hbm],
        out_specs=hbm,
        scratch_shapes=[
            pltpu.VMEM(block, jnp.bfloat16),
            pltpu.VMEM(block, jnp.bfloat16),
            pltpu.VMEM(out_block, jnp.bfloat16),
            pltpu.VMEM(out_block, jnp.bfloat16),
            pltpu.SemaphoreType.DMA((2, frames)),
        ] + [pltpu.SemaphoreType.DMA((2,))] * 6,
        compiler_params=pltpu.CompilerParams(
            collective_id=0, has_side_effects=True, vmem_limit_bytes=60 * 1024 * 1024
        ),
        cost_estimate=pl.CostEstimate(flops=2 * 10**9, bytes_accessed=10**7, transcendentals=10**7),
    )(key_frames.T, reach.T, used, query.reshape(flat), key.reshape(flat), value.reshape(flat))
    return out.reshape(query.shape)


def solution(mesh):
    return jax.shard_map(
        local,
        mesh=mesh,
        in_specs=(
            P("frame", "row", None, None),
            P("frame", "row", None, None),
            P("frame", "row", None, None),
            P(),
            P(),
            P(),
        ),
        out_specs=P("frame", "row", None, None),
        check_vma=False,
    )
```

```python
import functools

import jax
import jax.numpy as jnp
from jax import lax
from jax.experimental import pallas as pl
from jax.experimental.pallas import tpu as pltpu
from jax.sharding import PartitionSpec as P


HEAD_DIM = 128
MESH = pl.DeviceIdType.MESH
NEG = -1e30


def body(frames, pairs, cols, slots, kf_ref, reach_ref, used_ref, q_ref, k_ref, v_ref, o_ref,
         buf_a, buf_b, out_a, out_b, near_recv, far_recv, main_send, rim_send, rim_recv, out_send, out_recv):
    me = lax.axis_index("frame")
    pair = lax.axis_index("row")
    core = lax.rem(me, 2)
    half = lax.rem(me // 2, 2)
    bufs, outs = (buf_a, buf_b), (out_a, out_b)
    keys = 3 * cols
    two = 2 * cols
    v_at, q_at = keys, 2 * keys
    has_rim = jnp.logical_or(
        jnp.logical_and(half == 1, pair < pairs - 1), jnp.logical_and(half == 0, pair > 0)
    )
    no_rim = jnp.logical_not(has_rim)
    rim_pair = jnp.where(half == 1, pair + 1, pair - 1)
    rim_frame = 4 * (me // 4) + 2 * (1 - half) + core
    rim_row = pl.multiple_of(half * cols, cols)

    def head_of(device, slot):
        return 3 * (device // 4) + (2 * lax.rem(device, 2) if slot == 0 else 1)

    def chip(step, sign):
        k = step // 2
        distance = k + k // 2 - 2 * (k // 2) * lax.rem(k, 2)
        x = lax.rem(me // 4 + 4 + sign * distance, 4)
        return 4 * x + 2 * lax.rem(half + 1 + step, 2)

    barrier = pltpu.get_barrier_semaphore()

    @pl.loop(1, frames)
    def _(d):
        pl.semaphore_signal(barrier, inc=1, device_id=(lax.rem(me + d, frames), pair), device_id_type=MESH)

    @pl.when(has_rim)
    def _():
        pl.semaphore_signal(barrier, inc=1, device_id=(rim_frame, rim_pair), device_id_type=MESH)

    def piece(ref, device, slot, row, at):
        lanes = pl.ds(pl.multiple_of(head_of(device, slot) * HEAD_DIM, HEAD_DIM), HEAD_DIM)
        return (
            ref.at[pl.ds(pl.multiple_of(row * cols, cols), cols), lanes],
            bufs[slot].at[me, pl.ds(pl.multiple_of(at * cols, cols), cols)],
        )

    def half_of(device):
        return lax.rem(device // 2, 2)

    def near(device, slot):
        row = half_of(device)
        return piece(k_ref, device, slot, row, row), piece(v_ref, device, slot, row, 3 + row)

    def far(device, slot):
        row = 1 - half_of(device)
        return (
            piece(k_ref, device, slot, row, row),
            piece(v_ref, device, slot, row, 3 + row),
            piece(q_ref, device, slot, 1 - row, 6),
        )

    def keep(slot):
        for src, dst in near(me, slot):
            pltpu.make_async_copy(src, dst, near_recv.at[slot, me]).start()
        for src, dst in far(me, slot):
            pltpu.make_async_copy(src, dst, far_recv.at[slot]).start()

    def send(pieces, slot, recv_sem, device):
        for src, dst in pieces:
            pltpu.make_async_remote_copy(
                src_ref=src, dst_ref=dst, send_sem=main_send.at[slot], recv_sem=recv_sem,
                device_id=(device, pair), device_id_type=MESH,
            ).start()

    def settle(view, sem):
        pltpu.make_async_copy(view, view, sem).wait()

    keep(0)

    @pl.when(core == 0)
    def _():
        keep(1)

    @pl.when(has_rim)
    def _():
        pl.semaphore_wait(barrier, frames)

    @pl.when(no_rim)
    def _():
        pl.semaphore_wait(barrier, frames - 1)

    def each(slot, act):
        @pl.loop(0, frames // 2)
        def _(step):
            for c in range(2 - slot):
                device = chip(step, 1) + c

                @pl.when(device != me)
                def _():
                    act(device)

    for slot in range(2):
        each(slot, lambda device: send(near(device, slot), slot, near_recv.at[slot, me], device))
    for slot in range(2):
        each(slot, lambda device: send(far(device, slot), slot, far_recv.at[slot], device))

    def pass_rim(frame, slot):
        buf = bufs[slot]
        settle(buf.at[frame, pl.ds(0, two)], near_recv.at[slot, frame])

        @pl.when(has_rim)
        def _():
            for base in (0, v_at):
                pltpu.make_async_remote_copy(
                    src_ref=buf.at[frame, pl.ds(pl.multiple_of(base + rim_row, cols), cols)],
                    dst_ref=buf.at[frame, pl.ds(base + two, cols)],
                    send_sem=rim_send.at[slot], recv_sem=rim_recv.at[slot],
                    device_id=(rim_frame, rim_pair), device_id_type=MESH,
                ).start()

    def pass_rims(step, slot):
        for c in range(2):
            pass_rim(chip(step, -1) + c, slot)

    def clear_rim(slot):
        @pl.loop(0, frames)
        def _(frame):
            for base in (0, v_at):
                bufs[slot][frame, pl.ds(base + two, cols), :] = jnp.zeros((cols, HEAD_DIM), jnp.bfloat16)

    def wait_rest(slot):
        settle(bufs[slot].at[:, pl.ds(0, keys)], far_recv.at[slot])

        @pl.when(has_rim)
        def _():
            settle(bufs[slot].at[:, pl.ds(0, two)], rim_recv.at[slot])

    key_row = lax.broadcasted_iota(jnp.int32, (1, keys), 1) // cols
    distance = jnp.where(key_row == half, 0, 1)
    distance = jnp.where(jnp.logical_and(key_row == 2, no_rim), 9, distance)
    factor = HEAD_DIM ** -0.5 * 1.4426950408889634

    def spreads(frame):
        targets = [kf_ref[j, frame] for j in range(slots)]
        spans = [jnp.where(j < used_ref[frame], reach_ref[j, frame], -1) for j in range(slots)]
        found = []
        for j in range(slots):
            spread = spans[j]
            for i in range(slots):
                if i != j:
                    spread = jnp.maximum(spread, jnp.where(targets[i] == targets[j], spans[i], -1))
            for i in range(j):
                spread = jnp.where(jnp.logical_and(targets[i] == targets[j], spans[i] >= 0), -1, spread)
            found.append(jnp.where(spans[j] >= 0, spread, -1))
        return targets, found

    def attend(group, slot):
        buf = bufs[slot]
        masks = [spreads(frame) for frame in group]
        scores = [
            [
                lax.dot_general(
                    buf[frame, pl.ds(q_at, cols), :], buf[target, pl.ds(0, keys), :],
                    (((1,), (1,)), ((), ())), preferred_element_type=jnp.float32,
                )
                for target in targets
            ]
            for frame, (targets, _) in zip(group, masks)
        ]
        weights, totals = [], []
        for row, (_, found) in zip(scores, masks):
            row = [s * factor + jnp.where(distance <= spread, 0.0, NEG) for s, spread in zip(row, found)]
            peak = jnp.max(functools.reduce(jnp.maximum, row), axis=1, keepdims=True)
            row = [jnp.exp2(s - peak) for s in row]
            totals.append(jnp.sum(functools.reduce(jnp.add, row), axis=1, keepdims=True))
            weights.append(row)
        mixed = [
            functools.reduce(jnp.add, [
                lax.dot_general(
                    w.astype(jnp.bfloat16), buf[target, pl.ds(v_at, keys), :],
                    (((1,), (0,)), ((), ())), preferred_element_type=jnp.float32,
                )
                for w, target in zip(row, targets)
            ])
            for row, (targets, _) in zip(weights, masks)
        ]
        for frame, value, total in zip(group, mixed, totals):
            outs[slot][frame] = (value / total).astype(jnp.bfloat16)

    out_col = [pl.multiple_of(head_of(me, slot) * HEAD_DIM, HEAD_DIM) for slot in range(2)]
    out_row = pl.multiple_of(half * cols, cols)

    def send_out(frame, slot):
        view = o_ref.at[pl.ds(out_row, cols), pl.ds(out_col[slot], HEAD_DIM)]

        @pl.when(frame == me)
        def _():
            pltpu.make_async_copy(outs[slot].at[frame], view, out_recv.at[slot]).start()

        @pl.when(frame != me)
        def _():
            pltpu.make_async_remote_copy(
                src_ref=outs[slot].at[frame], dst_ref=view, send_sem=out_send.at[slot], recv_sem=out_recv.at[slot],
                device_id=(frame, pair), device_id_type=MESH,
            ).start()

    def work(step, slot):
        group = [lax.rem(me + 4 * step + u, frames) for u in range(4)]
        attend(group, slot)
        for frame in group:
            send_out(frame, slot)

    @pl.when(no_rim)
    def _():
        clear_rim(0)
        clear_rim(1)

    @pl.loop(0, frames // 2)
    def _(step):
        pass_rims(step, 0)

    @pl.when(core == 0)
    def _():
        @pl.loop(0, frames // 2)
        def _(step):
            pass_rims(step, 1)

    wait_rest(0)

    @pl.loop(0, frames // 4)
    def _(step):
        work(step, 0)

    @pl.when(core == 0)
    def _():
        wait_rest(1)

        @pl.loop(0, frames // 4)
        def _(step):
            work(step, 1)

    settle(buf_a.at[pl.ds(0, frames - 1), pl.ds(0, 2 * two + cols)], main_send.at[0])
    settle(out_a.at[pl.ds(0, frames - 1)], out_send.at[0])

    @pl.when(has_rim)
    def _():
        settle(buf_a.at[:, pl.ds(0, two)], rim_send.at[0])

    @pl.when(core == 0)
    def _():
        settle(buf_b.at[pl.ds(0, frames // 2 - 1), pl.ds(0, 2 * two + cols)], main_send.at[1])
        settle(out_b.at[pl.ds(0, frames - 1)], out_send.at[1])

        @pl.when(has_rim)
        def _():
            settle(buf_b.at[:, pl.ds(0, two)], rim_send.at[1])

    @pl.when(core == 1)
    def _():
        settle(buf_b.at[pl.ds(0, frames // 2), pl.ds(0, 2 * two + cols)], main_send.at[1])

    settle(out_a, out_recv.at[0])
    settle(out_b.at[pl.ds(0, frames // 2)], out_recv.at[1])


def local(query, key, value, key_frames, reach, used):
    _, rows, cols, features = query.shape
    frames, pairs = lax.axis_size("frame"), lax.axis_size("row")
    slots = key_frames.shape[1]
    flat = (rows * cols, features)
    block = (frames, 7 * cols, HEAD_DIM)
    out_block = (frames, cols, HEAD_DIM)
    smem = pl.BlockSpec(memory_space=pltpu.SMEM)
    hbm = pl.BlockSpec(memory_space=pl.ANY)
    out = pl.pallas_call(
        functools.partial(body, frames, pairs, cols, slots),
        out_shape=jax.ShapeDtypeStruct(flat, jnp.bfloat16),
        in_specs=[smem, smem, smem, hbm, hbm, hbm],
        out_specs=hbm,
        scratch_shapes=[
            pltpu.VMEM(block, jnp.bfloat16),
            pltpu.VMEM(block, jnp.bfloat16),
            pltpu.VMEM(out_block, jnp.bfloat16),
            pltpu.VMEM(out_block, jnp.bfloat16),
            pltpu.SemaphoreType.DMA((2, frames)),
        ] + [pltpu.SemaphoreType.DMA((2,))] * 6,
        compiler_params=pltpu.CompilerParams(
            collective_id=0, has_side_effects=True, vmem_limit_bytes=60 * 1024 * 1024
        ),
        cost_estimate=pl.CostEstimate(flops=2 * 10**9, bytes_accessed=10**7, transcendentals=10**7),
    )(key_frames.T, reach.T, used, query.reshape(flat), key.reshape(flat), value.reshape(flat))
    return out.reshape(query.shape)


def solution(mesh):
    return jax.shard_map(
        local,
        mesh=mesh,
        in_specs=(
            P("frame", "row", None, None),
            P("frame", "row", None, None),
            P("frame", "row", None, None),
            P(),
            P(),
            P(),
        ),
        out_specs=P("frame", "row", None, None),
        check_vma=False,
    )
```

```python
import functools

import jax
import jax.numpy as jnp
from jax import lax
from jax.experimental import pallas as pl
from jax.experimental.pallas import tpu as pltpu
from jax.sharding import PartitionSpec as P


HEAD_DIM = 128
MESH = pl.DeviceIdType.MESH
NEG = -1e30
GROUP = 8


def body(frames, pairs, cols, slots, kf_ref, reach_ref, used_ref, q_ref, k_ref, v_ref, o_ref,
         buf_a, buf_b, out_a, out_b, near_recv, far_recv, main_send, rim_send, rim_recv, out_send, out_recv):
    me = lax.axis_index("frame")
    pair = lax.axis_index("row")
    core = lax.rem(me, 2)
    half = lax.rem(me // 2, 2)
    bufs, outs = (buf_a, buf_b), (out_a, out_b)
    keys = 3 * cols
    two = 2 * cols
    v_at, q_at = keys, 2 * keys
    has_rim = jnp.logical_or(
        jnp.logical_and(half == 1, pair < pairs - 1), jnp.logical_and(half == 0, pair > 0)
    )
    no_rim = jnp.logical_not(has_rim)
    rim_pair = jnp.where(half == 1, pair + 1, pair - 1)
    rim_frame = 4 * (me // 4) + 2 * (1 - half) + core
    rim_row = pl.multiple_of(half * cols, cols)

    def head_of(device, slot):
        return 3 * (device // 4) + (2 * lax.rem(device, 2) if slot == 0 else 1)

    def chip(step, sign):
        k = step // 2
        distance = k + k // 2 - 2 * (k // 2) * lax.rem(k, 2)
        x = lax.rem(me // 4 + 4 + sign * distance, 4)
        return 4 * x + 2 * lax.rem(half + 1 + step, 2)

    barrier = pltpu.get_barrier_semaphore()

    @pl.loop(1, frames)
    def _(d):
        pl.semaphore_signal(barrier, inc=1, device_id=(lax.rem(me + d, frames), pair), device_id_type=MESH)

    @pl.when(has_rim)
    def _():
        pl.semaphore_signal(barrier, inc=1, device_id=(rim_frame, rim_pair), device_id_type=MESH)

    def piece(ref, device, slot, row, at):
        lanes = pl.ds(pl.multiple_of(head_of(device, slot) * HEAD_DIM, HEAD_DIM), HEAD_DIM)
        return (
            ref.at[pl.ds(pl.multiple_of(row * cols, cols), cols), lanes],
            bufs[slot].at[me, pl.ds(pl.multiple_of(at * cols, cols), cols)],
        )

    def half_of(device):
        return lax.rem(device // 2, 2)

    def near(device, slot):
        row = half_of(device)
        return piece(k_ref, device, slot, row, row), piece(v_ref, device, slot, row, 3 + row)

    def far(device, slot):
        row = 1 - half_of(device)
        return (
            piece(k_ref, device, slot, row, row),
            piece(v_ref, device, slot, row, 3 + row),
            piece(q_ref, device, slot, 1 - row, 6),
        )

    def keep(slot):
        for src, dst in near(me, slot):
            pltpu.make_async_copy(src, dst, near_recv.at[slot, me]).start()
        for src, dst in far(me, slot):
            pltpu.make_async_copy(src, dst, far_recv.at[slot]).start()

    def send(pieces, slot, recv_sem, device):
        for src, dst in pieces:
            pltpu.make_async_remote_copy(
                src_ref=src, dst_ref=dst, send_sem=main_send.at[slot], recv_sem=recv_sem,
                device_id=(device, pair), device_id_type=MESH,
            ).start()

    def settle(view, sem):
        pltpu.make_async_copy(view, view, sem).wait()

    keep(0)

    @pl.when(core == 0)
    def _():
        keep(1)

    @pl.when(has_rim)
    def _():
        pl.semaphore_wait(barrier, frames)

    @pl.when(no_rim)
    def _():
        pl.semaphore_wait(barrier, frames - 1)

    steps = frames // 2

    def send_near(step, slot):
        for c in range(2 - slot):
            device = chip(step, 1) + c

            @pl.when(device != me)
            def _():
                send(near(device, slot), slot, near_recv.at[slot, me], device)

    def send_far(step, slot):
        for c in range(2 - slot):
            device = chip(step, 1) + c

            @pl.when(device != me)
            def _():
                send(far(device, slot), slot, far_recv.at[slot], device)

    for slot in range(2):
        @pl.loop(0, steps)
        def _(step):
            send_near(step, slot)

    def pass_rim(frame, slot):
        buf = bufs[slot]
        settle(buf.at[frame, pl.ds(0, two)], near_recv.at[slot, frame])

        @pl.when(has_rim)
        def _():
            for base in (0, v_at):
                pltpu.make_async_remote_copy(
                    src_ref=buf.at[frame, pl.ds(pl.multiple_of(base + rim_row, cols), cols)],
                    dst_ref=buf.at[frame, pl.ds(base + two, cols)],
                    send_sem=rim_send.at[slot], recv_sem=rim_recv.at[slot],
                    device_id=(rim_frame, rim_pair), device_id_type=MESH,
                ).start()

    def pass_rims(step, slot):
        for c in range(2):
            pass_rim(chip(step, -1) + c, slot)

    def clear_rim(slot):
        @pl.loop(0, frames)
        def _(frame):
            for base in (0, v_at):
                bufs[slot][frame, pl.ds(base + two, cols), :] = jnp.zeros((cols, HEAD_DIM), jnp.bfloat16)

    def wait_rest(slot):
        settle(bufs[slot].at[:, pl.ds(0, keys)], far_recv.at[slot])

        @pl.when(has_rim)
        def _():
            settle(bufs[slot].at[:, pl.ds(0, two)], rim_recv.at[slot])

    key_row = lax.broadcasted_iota(jnp.int32, (1, keys), 1) // cols
    distance = jnp.where(key_row == half, 0, 1)
    distance = jnp.where(jnp.logical_and(key_row == 2, no_rim), 9, distance)
    factor = HEAD_DIM ** -0.5 * 1.4426950408889634

    def spreads(frame):
        targets = [kf_ref[j, frame] for j in range(slots)]
        spans = [jnp.where(j < used_ref[frame], reach_ref[j, frame], -1) for j in range(slots)]
        found = []
        for j in range(slots):
            spread = spans[j]
            for i in range(slots):
                if i != j:
                    spread = jnp.maximum(spread, jnp.where(targets[i] == targets[j], spans[i], -1))
            for i in range(j):
                spread = jnp.where(jnp.logical_and(targets[i] == targets[j], spans[i] >= 0), -1, spread)
            found.append(jnp.where(spans[j] >= 0, spread, -1))
        return targets, found

    def attend(group, slot):
        buf = bufs[slot]
        masks = [spreads(frame) for frame in group]
        scores = [
            [
                lax.dot_general(
                    buf[frame, pl.ds(q_at, cols), :], buf[target, pl.ds(0, keys), :],
                    (((1,), (1,)), ((), ())), preferred_element_type=jnp.float32,
                )
                for target in targets
            ]
            for frame, (targets, _) in zip(group, masks)
        ]
        weights, totals = [], []
        for row, (_, found) in zip(scores, masks):
            row = [s * factor + jnp.where(distance <= spread, 0.0, NEG) for s, spread in zip(row, found)]
            peak = jnp.max(functools.reduce(jnp.maximum, row), axis=1, keepdims=True)
            row = [jnp.exp2(s - peak) for s in row]
            totals.append(jnp.sum(functools.reduce(jnp.add, row), axis=1, keepdims=True))
            weights.append(row)
        mixed = [
            functools.reduce(jnp.add, [
                lax.dot_general(
                    w.astype(jnp.bfloat16), buf[target, pl.ds(v_at, keys), :],
                    (((1,), (0,)), ((), ())), preferred_element_type=jnp.float32,
                )
                for w, target in zip(row, targets)
            ])
            for row, (targets, _) in zip(weights, masks)
        ]
        for frame, value, total in zip(group, mixed, totals):
            outs[slot][frame] = (value / total).astype(jnp.bfloat16)

    out_col = [pl.multiple_of(head_of(me, slot) * HEAD_DIM, HEAD_DIM) for slot in range(2)]
    out_row = pl.multiple_of(half * cols, cols)

    def send_out(frame, slot):
        view = o_ref.at[pl.ds(out_row, cols), pl.ds(out_col[slot], HEAD_DIM)]

        @pl.when(frame == me)
        def _():
            pltpu.make_async_copy(outs[slot].at[frame], view, out_recv.at[slot]).start()

        @pl.when(frame != me)
        def _():
            pltpu.make_async_remote_copy(
                src_ref=outs[slot].at[frame], dst_ref=view, send_sem=out_send.at[slot], recv_sem=out_recv.at[slot],
                device_id=(frame, pair), device_id_type=MESH,
            ).start()

    def group_of(step):
        return [lax.rem(me + GROUP * step + u, frames) for u in range(GROUP)]

    @pl.when(no_rim)
    def _():
        clear_rim(0)
        clear_rim(1)

    @pl.loop(0, steps)
    def _(step):
        pass_rims(step, 0)
        send_far(step, 0)

    @pl.loop(0, steps)
    def _(step):
        send_far(step, 1)

        @pl.when(core == 0)
        def _():
            pass_rims(step, 1)

    wait_rest(0)

    @pl.loop(0, frames // GROUP)
    def _(step):
        attend(group_of(step), 0)

    @pl.loop(0, frames)
    def _(step):
        send_out(lax.rem(me + step, frames), 0)

    @pl.when(core == 0)
    def _():
        wait_rest(1)

        @pl.loop(0, frames // GROUP)
        def _(step):
            attend(group_of(step), 1)
            for frame in group_of(step):
                send_out(frame, 1)

    settle(buf_a.at[pl.ds(0, frames - 1), pl.ds(0, 2 * two + cols)], main_send.at[0])
    settle(out_a.at[pl.ds(0, frames - 1)], out_send.at[0])

    @pl.when(has_rim)
    def _():
        settle(buf_a.at[:, pl.ds(0, two)], rim_send.at[0])

    @pl.when(core == 0)
    def _():
        settle(buf_b.at[pl.ds(0, frames // 2 - 1), pl.ds(0, 2 * two + cols)], main_send.at[1])
        settle(out_b.at[pl.ds(0, frames - 1)], out_send.at[1])

        @pl.when(has_rim)
        def _():
            settle(buf_b.at[:, pl.ds(0, two)], rim_send.at[1])

    @pl.when(core == 1)
    def _():
        settle(buf_b.at[pl.ds(0, frames // 2), pl.ds(0, 2 * two + cols)], main_send.at[1])

    settle(out_a, out_recv.at[0])
    settle(out_b.at[pl.ds(0, frames // 2)], out_recv.at[1])


def local(query, key, value, key_frames, reach, used):
    _, rows, cols, features = query.shape
    frames, pairs = lax.axis_size("frame"), lax.axis_size("row")
    slots = key_frames.shape[1]
    flat = (rows * cols, features)
    block = (frames, 7 * cols, HEAD_DIM)
    out_block = (frames, cols, HEAD_DIM)
    smem = pl.BlockSpec(memory_space=pltpu.SMEM)
    hbm = pl.BlockSpec(memory_space=pl.ANY)
    out = pl.pallas_call(
        functools.partial(body, frames, pairs, cols, slots),
        out_shape=jax.ShapeDtypeStruct(flat, jnp.bfloat16),
        in_specs=[smem, smem, smem, hbm, hbm, hbm],
        out_specs=hbm,
        scratch_shapes=[
            pltpu.VMEM(block, jnp.bfloat16),
            pltpu.VMEM(block, jnp.bfloat16),
            pltpu.VMEM(out_block, jnp.bfloat16),
            pltpu.VMEM(out_block, jnp.bfloat16),
            pltpu.SemaphoreType.DMA((2, frames)),
        ] + [pltpu.SemaphoreType.DMA((2,))] * 6,
        compiler_params=pltpu.CompilerParams(
            collective_id=0, has_side_effects=True, vmem_limit_bytes=53 * 1024 * 1024
        ),
        cost_estimate=pl.CostEstimate(flops=2 * 10**9, bytes_accessed=10**7, transcendentals=10**7),
    )(key_frames.T, reach.T, used, query.reshape(flat), key.reshape(flat), value.reshape(flat))
    return out.reshape(query.shape)


def solution(mesh):
    return jax.shard_map(
        local,
        mesh=mesh,
        in_specs=(
            P("frame", "row", None, None),
            P("frame", "row", None, None),
            P("frame", "row", None, None),
            P(),
            P(),
            P(),
        ),
        out_specs=P("frame", "row", None, None),
        check_vma=False,
    )
```

```python
import functools

import jax
import jax.numpy as jnp
from jax import lax
from jax.experimental import pallas as pl
from jax.experimental.pallas import tpu as pltpu
from jax.sharding import PartitionSpec as P


HEAD_DIM = 128
MESH = pl.DeviceIdType.MESH
NEG = -1e30
GROUPS = (8, 4)


def body(frames, pairs, cols, slots, kf_hbm, reach_hbm, used_hbm, q_ref, k_ref, v_ref, o_ref,
         buf_a, buf_b, out_a, out_b, near_recv, far_recv, main_send, rim_send, rim_recv, out_send, out_recv, kf_ref, reach_ref, used_ref, mask_sem):
    me = lax.axis_index("frame")
    pair = lax.axis_index("row")
    core = lax.rem(me, 2)
    half = lax.rem(me // 2, 2)
    bufs, outs = (buf_a, buf_b), (out_a, out_b)
    keys = 3 * cols
    two = 2 * cols
    v_at, q_at = keys, 2 * keys
    has_rim = jnp.logical_or(
        jnp.logical_and(half == 1, pair < pairs - 1), jnp.logical_and(half == 0, pair > 0)
    )
    no_rim = jnp.logical_not(has_rim)
    rim_pair = jnp.where(half == 1, pair + 1, pair - 1)
    rim_frame = 4 * (me // 4) + 2 * (1 - half) + core
    rim_row = pl.multiple_of(half * cols, cols)

    def head_of(device, slot):
        return 3 * (device // 4) + (2 * lax.rem(device, 2) if slot == 0 else 1)

    def chip(step, sign):
        k = step // 2
        distance = k + k // 2 - 2 * (k // 2) * lax.rem(k, 2)
        x = lax.rem(me // 4 + 4 + sign * distance, 4)
        return 4 * x + 2 * lax.rem(half + 1 + step, 2)

    mask_copies = [
        pltpu.make_async_copy(src, dst, mask_sem.at[i])
        for i, (src, dst) in enumerate(((kf_hbm, kf_ref), (reach_hbm, reach_ref), (used_hbm, used_ref)))
    ]
    for copy in mask_copies:
        copy.start()

    barrier = pltpu.get_barrier_semaphore()

    @pl.loop(1, frames)
    def _(d):
        pl.semaphore_signal(barrier, inc=1, device_id=(lax.rem(me + d, frames), pair), device_id_type=MESH)

    @pl.when(has_rim)
    def _():
        pl.semaphore_signal(barrier, inc=1, device_id=(rim_frame, rim_pair), device_id_type=MESH)

    def piece(ref, device, slot, row, at):
        lanes = pl.ds(pl.multiple_of(head_of(device, slot) * HEAD_DIM, HEAD_DIM), HEAD_DIM)
        return (
            ref.at[pl.ds(pl.multiple_of(row * cols, cols), cols), lanes],
            bufs[slot].at[me, pl.ds(pl.multiple_of(at * cols, cols), cols)],
        )

    def half_of(device):
        return lax.rem(device // 2, 2)

    def near(device, slot):
        row = half_of(device)
        return piece(k_ref, device, slot, row, row), piece(v_ref, device, slot, row, 3 + row)

    def far(device, slot):
        row = 1 - half_of(device)
        return (
            piece(k_ref, device, slot, row, row),
            piece(v_ref, device, slot, row, 3 + row),
            piece(q_ref, device, slot, 1 - row, 6),
        )

    def keep(slot):
        for src, dst in near(me, slot):
            pltpu.make_async_copy(src, dst, near_recv.at[slot, me]).start()
        for src, dst in far(me, slot):
            pltpu.make_async_copy(src, dst, far_recv.at[slot]).start()

    def send(pieces, slot, recv_sem, device):
        for src, dst in pieces:
            pltpu.make_async_remote_copy(
                src_ref=src, dst_ref=dst, send_sem=main_send.at[slot], recv_sem=recv_sem,
                device_id=(device, pair), device_id_type=MESH,
            ).start()

    def settle(view, sem):
        pltpu.make_async_copy(view, view, sem).wait()

    keep(0)

    @pl.when(core == 0)
    def _():
        keep(1)

    @pl.when(has_rim)
    def _():
        pl.semaphore_wait(barrier, frames)

    @pl.when(no_rim)
    def _():
        pl.semaphore_wait(barrier, frames - 1)

    steps = frames // 2

    def send_near(step, slot):
        for c in range(2 - slot):
            device = chip(step, 1) + c

            @pl.when(device != me)
            def _():
                send(near(device, slot), slot, near_recv.at[slot, me], device)

    def send_far(step, slot):
        for c in range(2 - slot):
            device = chip(step, 1) + c

            @pl.when(device != me)
            def _():
                send(far(device, slot), slot, far_recv.at[slot], device)

    for slot in range(2):
        @pl.loop(0, steps)
        def _(step):
            send_near(step, slot)

    def pass_rim(frame, slot):
        buf = bufs[slot]
        settle(buf.at[frame, pl.ds(0, two)], near_recv.at[slot, frame])

        @pl.when(has_rim)
        def _():
            for base in (0, v_at):
                pltpu.make_async_remote_copy(
                    src_ref=buf.at[frame, pl.ds(pl.multiple_of(base + rim_row, cols), cols)],
                    dst_ref=buf.at[frame, pl.ds(base + two, cols)],
                    send_sem=rim_send.at[slot], recv_sem=rim_recv.at[slot],
                    device_id=(rim_frame, rim_pair), device_id_type=MESH,
                ).start()

    def pass_rims(step, slot):
        for c in range(2):
            pass_rim(chip(step, -1) + c, slot)

    def clear_rim(slot):
        @pl.loop(0, frames)
        def _(frame):
            for base in (0, v_at):
                bufs[slot][frame, pl.ds(base + two, cols), :] = jnp.zeros((cols, HEAD_DIM), jnp.bfloat16)

    def wait_rest(slot):
        settle(bufs[slot].at[:, pl.ds(0, keys)], far_recv.at[slot])

        @pl.when(has_rim)
        def _():
            settle(bufs[slot].at[:, pl.ds(0, two)], rim_recv.at[slot])

    key_row = lax.broadcasted_iota(jnp.int32, (1, keys), 1) // cols
    distance = jnp.where(key_row == half, 0, 1)
    distance = jnp.where(jnp.logical_and(key_row == 2, no_rim), 9, distance)
    factor = HEAD_DIM ** -0.5 * 1.4426950408889634

    def spreads(frame):
        targets = [kf_ref[j, frame] for j in range(slots)]
        spans = [jnp.where(j < used_ref[frame], reach_ref[j, frame], -1) for j in range(slots)]
        found = []
        for j in range(slots):
            spread = spans[j]
            for i in range(slots):
                if i != j:
                    spread = jnp.maximum(spread, jnp.where(targets[i] == targets[j], spans[i], -1))
            for i in range(j):
                spread = jnp.where(jnp.logical_and(targets[i] == targets[j], spans[i] >= 0), -1, spread)
            found.append(jnp.where(spans[j] >= 0, spread, -1))
        return targets, found

    def attend(group, slot):
        buf = bufs[slot]
        masks = [spreads(frame) for frame in group]
        scores = [
            [
                lax.dot_general(
                    buf[frame, pl.ds(q_at, cols), :], buf[target, pl.ds(0, keys), :],
                    (((1,), (1,)), ((), ())), preferred_element_type=jnp.float32,
                )
                for target in targets
            ]
            for frame, (targets, _) in zip(group, masks)
        ]
        weights, totals = [], []
        for row, (_, found) in zip(scores, masks):
            row = [s * factor + jnp.where(distance <= spread, 0.0, NEG) for s, spread in zip(row, found)]
            peak = jnp.max(functools.reduce(jnp.maximum, row), axis=1, keepdims=True)
            row = [jnp.exp2(s - peak) for s in row]
            totals.append(jnp.sum(functools.reduce(jnp.add, row), axis=1, keepdims=True))
            weights.append(row)
        mixed = [
            functools.reduce(jnp.add, [
                lax.dot_general(
                    w.astype(jnp.bfloat16), buf[target, pl.ds(v_at, keys), :],
                    (((1,), (0,)), ((), ())), preferred_element_type=jnp.float32,
                )
                for w, target in zip(row, targets)
            ])
            for row, (targets, _) in zip(weights, masks)
        ]
        for frame, value, total in zip(group, mixed, totals):
            outs[slot][frame] = (value / total).astype(jnp.bfloat16)

    out_col = [pl.multiple_of(head_of(me, slot) * HEAD_DIM, HEAD_DIM) for slot in range(2)]
    out_row = pl.multiple_of(half * cols, cols)

    def send_out(frame, slot):
        view = o_ref.at[pl.ds(out_row, cols), pl.ds(out_col[slot], HEAD_DIM)]

        @pl.when(frame == me)
        def _():
            pltpu.make_async_copy(outs[slot].at[frame], view, out_recv.at[slot]).start()

        @pl.when(frame != me)
        def _():
            pltpu.make_async_remote_copy(
                src_ref=outs[slot].at[frame], dst_ref=view, send_sem=out_send.at[slot], recv_sem=out_recv.at[slot],
                device_id=(frame, pair), device_id_type=MESH,
            ).start()

    def group_of(step, size):
        group = []
        for u in range(size // 2):
            t = size // 2 * step + u
            first = chip(6 - 4 * lax.rem(t, 2) - 2 * (lax.rem(t, 4) // 2) + t // 4, 1)
            group += [first, first + 1]
        return group

    @pl.when(no_rim)
    def _():
        clear_rim(0)
        clear_rim(1)

    @pl.loop(0, steps)
    def _(step):
        pass_rims(step, 0)
        send_far(step, 0)

    @pl.loop(0, steps)
    def _(step):
        send_far(step, 1)

        @pl.when(core == 0)
        def _():
            pass_rims(step, 1)

    for copy in mask_copies:
        copy.wait()

    wait_rest(0)

    @pl.loop(0, frames // GROUPS[0])
    def _(step):
        attend(group_of(step, GROUPS[0]), 0)

    @pl.loop(0, steps)
    def _(step):
        for frame in group_of(step, 2):
            send_out(frame, 0)

    @pl.when(core == 0)
    def _():
        wait_rest(1)

        @pl.loop(0, frames // GROUPS[1])
        def _(step):
            group = group_of(step, GROUPS[1])
            attend(group, 1)
            for frame in group:
                send_out(frame, 1)

    settle(buf_a.at[pl.ds(0, frames - 1), pl.ds(0, 2 * two + cols)], main_send.at[0])
    settle(out_a.at[pl.ds(0, frames - 1)], out_send.at[0])

    @pl.when(has_rim)
    def _():
        settle(buf_a.at[:, pl.ds(0, two)], rim_send.at[0])

    @pl.when(core == 0)
    def _():
        settle(buf_b.at[pl.ds(0, frames // 2 - 1), pl.ds(0, 2 * two + cols)], main_send.at[1])
        settle(out_b.at[pl.ds(0, frames - 1)], out_send.at[1])

        @pl.when(has_rim)
        def _():
            settle(buf_b.at[:, pl.ds(0, two)], rim_send.at[1])

    @pl.when(core == 1)
    def _():
        settle(buf_b.at[pl.ds(0, frames // 2), pl.ds(0, 2 * two + cols)], main_send.at[1])

    settle(out_a, out_recv.at[0])
    settle(out_b.at[pl.ds(0, frames // 2)], out_recv.at[1])


def local(query, key, value, key_frames, reach, used):
    _, rows, cols, features = query.shape
    frames, pairs = lax.axis_size("frame"), lax.axis_size("row")
    slots = key_frames.shape[1]
    flat = (rows * cols, features)
    block = (frames, 7 * cols, HEAD_DIM)
    out_block = (frames, cols, HEAD_DIM)
    hbm = pl.BlockSpec(memory_space=pl.ANY)
    out = pl.pallas_call(
        functools.partial(body, frames, pairs, cols, slots),
        out_shape=jax.ShapeDtypeStruct(flat, jnp.bfloat16),
        in_specs=[hbm] * 6,
        out_specs=hbm,
        scratch_shapes=[
            pltpu.VMEM(block, jnp.bfloat16),
            pltpu.VMEM(block, jnp.bfloat16),
            pltpu.VMEM(out_block, jnp.bfloat16),
            pltpu.VMEM(out_block, jnp.bfloat16),
            pltpu.SemaphoreType.DMA((2, frames)),
        ] + [pltpu.SemaphoreType.DMA((2,))] * 6 + [
            pltpu.SMEM((slots, frames), jnp.int32),
            pltpu.SMEM((slots, frames), jnp.int32),
            pltpu.SMEM((frames,), jnp.int32),
            pltpu.SemaphoreType.DMA((3,)),
        ],
        compiler_params=pltpu.CompilerParams(
            collective_id=0, has_side_effects=True, vmem_limit_bytes=53 * 1024 * 1024
        ),
        cost_estimate=pl.CostEstimate(flops=2 * 10**9, bytes_accessed=10**7, transcendentals=10**7),
    )(key_frames.T, reach.T, used, query.reshape(flat), key.reshape(flat), value.reshape(flat))
    return out.reshape(query.shape)


def solution(mesh):
    return jax.shard_map(
        local,
        mesh=mesh,
        in_specs=(
            P("frame", "row", None, None),
            P("frame", "row", None, None),
            P("frame", "row", None, None),
            P(),
            P(),
            P(),
        ),
        out_specs=P("frame", "row", None, None),
        check_vma=False,
    )
```

```python
import functools

import jax
import jax.numpy as jnp
from jax import lax
from jax.experimental import pallas as pl
from jax.experimental.pallas import tpu as pltpu
from jax.sharding import PartitionSpec as P


HEAD_DIM = 128
MESH = pl.DeviceIdType.MESH
NEG = -1e30
GROUPS = (8, 4)


def body(frames, pairs, cols, slots, kf_hbm, reach_hbm, used_hbm, q_ref, k_ref, v_ref, o_ref,
         buf_a, buf_b, out_a, out_b, near_recv, far_recv, main_send, rim_send, rim_recv, out_send, out_recv, kf_ref, reach_ref, used_ref, mask_sem):
    me = lax.axis_index("frame")
    pair = lax.axis_index("row")
    core = lax.rem(me, 2)
    half = lax.rem(me // 2, 2)
    bufs, outs = (buf_a, buf_b), (out_a, out_b)
    keys = 3 * cols
    two = 2 * cols
    q_at = 2 * keys
    has_rim = jnp.logical_or(
        jnp.logical_and(half == 1, pair < pairs - 1), jnp.logical_and(half == 0, pair > 0)
    )
    no_rim = jnp.logical_not(has_rim)
    rim_pair = jnp.where(half == 1, pair + 1, pair - 1)
    rim_frame = 4 * (me // 4) + 2 * (1 - half) + core
    rim_row = pl.multiple_of(half * two, two)

    def head_of(device, slot):
        return 3 * (device // 4) + (2 * lax.rem(device, 2) if slot == 0 else 1)

    def chip(step, sign):
        k = step // 2
        distance = k + k // 2 - 2 * (k // 2) * lax.rem(k, 2)
        x = lax.rem(me // 4 + 4 + sign * distance, 4)
        return 4 * x + 2 * lax.rem(half + 1 + step, 2)

    mask_copies = [
        pltpu.make_async_copy(src, dst, mask_sem.at[i])
        for i, (src, dst) in enumerate(((kf_hbm, kf_ref), (reach_hbm, reach_ref), (used_hbm, used_ref)))
    ]
    for copy in mask_copies:
        copy.start()

    barrier = pltpu.get_barrier_semaphore()

    @pl.loop(1, frames)
    def _(d):
        pl.semaphore_signal(barrier, inc=1, device_id=(lax.rem(me + d, frames), pair), device_id_type=MESH)

    @pl.when(has_rim)
    def _():
        pl.semaphore_signal(barrier, inc=1, device_id=(rim_frame, rim_pair), device_id_type=MESH)

    def piece(ref, device, slot, row, at):
        lanes = pl.ds(pl.multiple_of(head_of(device, slot) * HEAD_DIM, HEAD_DIM), HEAD_DIM)
        return (
            ref.at[pl.ds(pl.multiple_of(row * cols, cols), cols), lanes],
            bufs[slot].at[me, pl.ds(pl.multiple_of(at * cols, cols), cols)],
        )

    def half_of(device):
        return lax.rem(device // 2, 2)

    def near(device, slot):
        row = half_of(device)
        return piece(k_ref, device, slot, row, 2 * row), piece(v_ref, device, slot, row, 2 * row + 1)

    def far(device, slot):
        row = 1 - half_of(device)
        return (
            piece(k_ref, device, slot, row, 2 * row),
            piece(v_ref, device, slot, row, 2 * row + 1),
            piece(q_ref, device, slot, 1 - row, 6),
        )

    def keep(slot):
        for src, dst in near(me, slot):
            pltpu.make_async_copy(src, dst, near_recv.at[slot, me]).start()
        for src, dst in far(me, slot):
            pltpu.make_async_copy(src, dst, far_recv.at[slot]).start()

    def send(pieces, slot, recv_sem, device):
        for src, dst in pieces:
            pltpu.make_async_remote_copy(
                src_ref=src, dst_ref=dst, send_sem=main_send.at[slot], recv_sem=recv_sem,
                device_id=(device, pair), device_id_type=MESH,
            ).start()

    def settle(view, sem):
        pltpu.make_async_copy(view, view, sem).wait()

    keep(0)

    @pl.when(core == 0)
    def _():
        keep(1)

    @pl.when(has_rim)
    def _():
        pl.semaphore_wait(barrier, frames)

    @pl.when(no_rim)
    def _():
        pl.semaphore_wait(barrier, frames - 1)

    steps = frames // 2

    def send_near(step, slot):
        for c in range(2 - slot):
            device = chip(step, 1) + c

            @pl.when(device != me)
            def _():
                send(near(device, slot), slot, near_recv.at[slot, me], device)

    def send_far(step, slot):
        for c in range(2 - slot):
            device = chip(step, 1) + c

            @pl.when(device != me)
            def _():
                send(far(device, slot), slot, far_recv.at[slot], device)

    for slot in range(2):
        @pl.loop(0, steps)
        def _(step):
            send_near(step, slot)

    def pass_rim(frame, slot):
        buf = bufs[slot]
        settle(buf.at[frame, pl.ds(0, two)], near_recv.at[slot, frame])

        @pl.when(has_rim)
        def _():
            pltpu.make_async_remote_copy(
                src_ref=buf.at[frame, pl.ds(rim_row, two)], dst_ref=buf.at[frame, pl.ds(2 * two, two)],
                send_sem=rim_send.at[slot], recv_sem=rim_recv.at[slot],
                device_id=(rim_frame, rim_pair), device_id_type=MESH,
            ).start()

    def pass_rims(step, slot):
        for c in range(2):
            pass_rim(chip(step, -1) + c, slot)

    def clear_rim(slot):
        @pl.loop(0, frames)
        def _(frame):
            bufs[slot][frame, pl.ds(2 * two, two), :] = jnp.zeros((two, HEAD_DIM), jnp.bfloat16)

    def wait_rest(slot):
        settle(bufs[slot].at[:, pl.ds(0, keys)], far_recv.at[slot])

        @pl.when(has_rim)
        def _():
            settle(bufs[slot].at[:, pl.ds(0, two)], rim_recv.at[slot])

    key_row = lax.broadcasted_iota(jnp.int32, (1, keys), 1) // cols
    distance = jnp.where(key_row == half, 0, 1)
    distance = jnp.where(jnp.logical_and(key_row == 2, no_rim), 9, distance)
    factor = HEAD_DIM ** -0.5 * 1.4426950408889634

    def spreads(frame):
        targets = [kf_ref[j, frame] for j in range(slots)]
        spans = [jnp.where(j < used_ref[frame], reach_ref[j, frame], -1) for j in range(slots)]
        found = []
        for j in range(slots):
            spread = spans[j]
            for i in range(slots):
                if i != j:
                    spread = jnp.maximum(spread, jnp.where(targets[i] == targets[j], spans[i], -1))
            for i in range(j):
                spread = jnp.where(jnp.logical_and(targets[i] == targets[j], spans[i] >= 0), -1, spread)
            found.append(jnp.where(spans[j] >= 0, spread, -1))
        return targets, found

    def seen(buf, frame, which):
        return jnp.concatenate([buf[frame, pl.ds((2 * i + which) * cols, cols), :] for i in range(3)], axis=0)

    def attend(group, slot):
        buf = bufs[slot]
        masks = [spreads(frame) for frame in group]
        scores = [
            [
                lax.dot_general(
                    buf[frame, pl.ds(q_at, cols), :], seen(buf, target, 0),
                    (((1,), (1,)), ((), ())), preferred_element_type=jnp.float32,
                )
                for target in targets
            ]
            for frame, (targets, _) in zip(group, masks)
        ]
        weights, totals = [], []
        for row, (_, found) in zip(scores, masks):
            row = [s * factor + jnp.where(distance <= spread, 0.0, NEG) for s, spread in zip(row, found)]
            peak = jnp.max(functools.reduce(jnp.maximum, row), axis=1, keepdims=True)
            row = [jnp.exp2(s - peak) for s in row]
            totals.append(jnp.sum(functools.reduce(jnp.add, row), axis=1, keepdims=True))
            weights.append(row)
        mixed = [
            functools.reduce(jnp.add, [
                lax.dot_general(
                    w.astype(jnp.bfloat16), seen(buf, target, 1),
                    (((1,), (0,)), ((), ())), preferred_element_type=jnp.float32,
                )
                for w, target in zip(row, targets)
            ])
            for row, (targets, _) in zip(weights, masks)
        ]
        for frame, value, total in zip(group, mixed, totals):
            outs[slot][frame] = (value / total).astype(jnp.bfloat16)

    out_col = [pl.multiple_of(head_of(me, slot) * HEAD_DIM, HEAD_DIM) for slot in range(2)]
    out_row = pl.multiple_of(half * cols, cols)

    def send_out(frame, slot):
        view = o_ref.at[pl.ds(out_row, cols), pl.ds(out_col[slot], HEAD_DIM)]

        @pl.when(frame == me)
        def _():
            pltpu.make_async_copy(outs[slot].at[frame], view, out_recv.at[slot]).start()

        @pl.when(frame != me)
        def _():
            pltpu.make_async_remote_copy(
                src_ref=outs[slot].at[frame], dst_ref=view, send_sem=out_send.at[slot], recv_sem=out_recv.at[slot],
                device_id=(frame, pair), device_id_type=MESH,
            ).start()

    def group_of(step, size):
        group = []
        for u in range(size // 2):
            t = size // 2 * step + u
            first = chip(6 - 4 * lax.rem(t, 2) - 2 * (lax.rem(t, 4) // 2) + t // 4, 1)
            group += [first, first + 1]
        return group

    @pl.when(no_rim)
    def _():
        clear_rim(0)
        clear_rim(1)

    @pl.loop(0, steps)
    def _(step):
        pass_rims(step, 0)
        send_far(step, 0)

    @pl.loop(0, steps)
    def _(step):
        send_far(step, 1)

        @pl.when(core == 0)
        def _():
            pass_rims(step, 1)

    for copy in mask_copies:
        copy.wait()

    wait_rest(0)

    @pl.loop(0, frames // GROUPS[0])
    def _(step):
        attend(group_of(step, GROUPS[0]), 0)

    @pl.loop(0, steps)
    def _(step):
        for frame in group_of(step, 2):
            send_out(frame, 0)

    @pl.when(core == 0)
    def _():
        wait_rest(1)

        @pl.loop(0, frames // GROUPS[1])
        def _(step):
            group = group_of(step, GROUPS[1])
            attend(group, 1)
            for frame in group:
                send_out(frame, 1)

    settle(buf_a.at[pl.ds(0, frames - 1), pl.ds(0, 2 * two + cols)], main_send.at[0])
    settle(out_a.at[pl.ds(0, frames - 1)], out_send.at[0])

    @pl.when(has_rim)
    def _():
        settle(buf_a.at[:, pl.ds(0, two)], rim_send.at[0])

    @pl.when(core == 0)
    def _():
        settle(buf_b.at[pl.ds(0, frames // 2 - 1), pl.ds(0, 2 * two + cols)], main_send.at[1])
        settle(out_b.at[pl.ds(0, frames - 1)], out_send.at[1])

        @pl.when(has_rim)
        def _():
            settle(buf_b.at[:, pl.ds(0, two)], rim_send.at[1])

    @pl.when(core == 1)
    def _():
        settle(buf_b.at[pl.ds(0, frames // 2), pl.ds(0, 2 * two + cols)], main_send.at[1])

    settle(out_a, out_recv.at[0])
    settle(out_b.at[pl.ds(0, frames // 2)], out_recv.at[1])


def local(query, key, value, key_frames, reach, used):
    _, rows, cols, features = query.shape
    frames, pairs = lax.axis_size("frame"), lax.axis_size("row")
    slots = key_frames.shape[1]
    flat = (rows * cols, features)
    block = (frames, 7 * cols, HEAD_DIM)
    out_block = (frames, cols, HEAD_DIM)
    hbm = pl.BlockSpec(memory_space=pl.ANY)
    out = pl.pallas_call(
        functools.partial(body, frames, pairs, cols, slots),
        out_shape=jax.ShapeDtypeStruct(flat, jnp.bfloat16),
        in_specs=[hbm] * 6,
        out_specs=hbm,
        scratch_shapes=[
            pltpu.VMEM(block, jnp.bfloat16),
            pltpu.VMEM(block, jnp.bfloat16),
            pltpu.VMEM(out_block, jnp.bfloat16),
            pltpu.VMEM(out_block, jnp.bfloat16),
            pltpu.SemaphoreType.DMA((2, frames)),
        ] + [pltpu.SemaphoreType.DMA((2,))] * 6 + [
            pltpu.SMEM((slots, frames), jnp.int32),
            pltpu.SMEM((slots, frames), jnp.int32),
            pltpu.SMEM((frames,), jnp.int32),
            pltpu.SemaphoreType.DMA((3,)),
        ],
        compiler_params=pltpu.CompilerParams(
            collective_id=0, has_side_effects=True, vmem_limit_bytes=53 * 1024 * 1024
        ),
        cost_estimate=pl.CostEstimate(flops=2 * 10**9, bytes_accessed=10**7, transcendentals=10**7),
    )(key_frames.T, reach.T, used, query.reshape(flat), key.reshape(flat), value.reshape(flat))
    return out.reshape(query.shape)


def solution(mesh):
    return jax.shard_map(
        local,
        mesh=mesh,
        in_specs=(
            P("frame", "row", None, None),
            P("frame", "row", None, None),
            P("frame", "row", None, None),
            P(),
            P(),
            P(),
        ),
        out_specs=P("frame", "row", None, None),
        check_vma=False,
    )
```

```python
import functools

import jax
import jax.numpy as jnp
from jax import lax
from jax.experimental import pallas as pl
from jax.experimental.pallas import tpu as pltpu
from jax.sharding import PartitionSpec as P


HEAD_DIM = 128
MESH = pl.DeviceIdType.MESH
NEG = -1e30
LARGE_CORE = 1
GROUPS = (8, 4)


def body(frames, pairs, cols, slots, kf_hbm, reach_hbm, used_hbm, q_ref, k_ref, v_ref, o_ref,
         buf_a, buf_b, out_a, out_b, near_recv, far_recv, main_send, rim_send, rim_recv, out_send, out_recv, kf_ref, reach_ref, used_ref, mask_sem):
    me = lax.axis_index("frame")
    pair = lax.axis_index("row")
    core = lax.rem(me, 2)
    half = lax.rem(me // 2, 2)
    bufs, outs = (buf_a, buf_b), (out_a, out_b)
    keys = 3 * cols
    two = 2 * cols
    q_at = 2 * keys
    has_rim = jnp.logical_or(
        jnp.logical_and(half == 1, pair < pairs - 1), jnp.logical_and(half == 0, pair > 0)
    )
    no_rim = jnp.logical_not(has_rim)
    rim_pair = jnp.where(half == 1, pair + 1, pair - 1)
    rim_frame = 4 * (me // 4) + 2 * (1 - half) + core
    rim_row = pl.multiple_of(half * two, two)

    def head_of(device, slot):
        return 3 * (device // 4) + (2 * lax.rem(device + LARGE_CORE, 2) if slot == 0 else 1)

    def chip(step, sign):
        k = step // 2
        distance = k + k // 2 - 2 * (k // 2) * lax.rem(k, 2)
        x = lax.rem(me // 4 + 4 + sign * distance, 4)
        return 4 * x + 2 * lax.rem(half + 1 + step, 2)

    mask_copies = [
        pltpu.make_async_copy(src, dst, mask_sem.at[i])
        for i, (src, dst) in enumerate(((kf_hbm, kf_ref), (reach_hbm, reach_ref), (used_hbm, used_ref)))
    ]
    for copy in mask_copies:
        copy.start()

    barrier = pltpu.get_barrier_semaphore()

    @pl.loop(1, frames)
    def _(d):
        pl.semaphore_signal(barrier, inc=1, device_id=(lax.rem(me + d, frames), pair), device_id_type=MESH)

    @pl.when(has_rim)
    def _():
        pl.semaphore_signal(barrier, inc=1, device_id=(rim_frame, rim_pair), device_id_type=MESH)

    def piece(ref, device, slot, row, at):
        lanes = pl.ds(pl.multiple_of(head_of(device, slot) * HEAD_DIM, HEAD_DIM), HEAD_DIM)
        return (
            ref.at[pl.ds(pl.multiple_of(row * cols, cols), cols), lanes],
            bufs[slot].at[me, pl.ds(pl.multiple_of(at * cols, cols), cols)],
        )

    def half_of(device):
        return lax.rem(device // 2, 2)

    def near(device, slot):
        row = half_of(device)
        return piece(k_ref, device, slot, row, 2 * row), piece(v_ref, device, slot, row, 2 * row + 1)

    def far(device, slot):
        row = 1 - half_of(device)
        return (
            piece(k_ref, device, slot, row, 2 * row),
            piece(v_ref, device, slot, row, 2 * row + 1),
            piece(q_ref, device, slot, 1 - row, 6),
        )

    def keep(slot):
        for src, dst in near(me, slot):
            pltpu.make_async_copy(src, dst, near_recv.at[slot, me]).start()
        for src, dst in far(me, slot):
            pltpu.make_async_copy(src, dst, far_recv.at[slot]).start()

    def send(pieces, slot, recv_sem, device):
        for src, dst in pieces:
            pltpu.make_async_remote_copy(
                src_ref=src, dst_ref=dst, send_sem=main_send.at[slot], recv_sem=recv_sem,
                device_id=(device, pair), device_id_type=MESH,
            ).start()

    def settle(view, sem):
        pltpu.make_async_copy(view, view, sem).wait()

    keep(0)

    @pl.when(core == LARGE_CORE)
    def _():
        keep(1)

    @pl.when(has_rim)
    def _():
        pl.semaphore_wait(barrier, frames)

    @pl.when(no_rim)
    def _():
        pl.semaphore_wait(barrier, frames - 1)

    steps = frames // 2

    def send_near(step, slot):
        for c in range(2 - slot):
            device = chip(step, 1) + (c + LARGE_CORE) % 2

            @pl.when(device != me)
            def _():
                send(near(device, slot), slot, near_recv.at[slot, me], device)

    def send_far(step, slot):
        for c in range(2 - slot):
            device = chip(step, 1) + (c + LARGE_CORE) % 2

            @pl.when(device != me)
            def _():
                send(far(device, slot), slot, far_recv.at[slot], device)

    for slot in range(2):
        @pl.loop(0, steps)
        def _(step):
            send_near(step, slot)

    def pass_rim(frame, slot):
        buf = bufs[slot]
        settle(buf.at[frame, pl.ds(0, two)], near_recv.at[slot, frame])

        @pl.when(has_rim)
        def _():
            pltpu.make_async_remote_copy(
                src_ref=buf.at[frame, pl.ds(rim_row, two)], dst_ref=buf.at[frame, pl.ds(2 * two, two)],
                send_sem=rim_send.at[slot], recv_sem=rim_recv.at[slot],
                device_id=(rim_frame, rim_pair), device_id_type=MESH,
            ).start()

    def pass_rims(step, slot):
        for c in range(2):
            pass_rim(chip(step, -1) + c, slot)

    def clear_rim(slot):
        @pl.loop(0, frames)
        def _(frame):
            bufs[slot][frame, pl.ds(2 * two, two), :] = jnp.zeros((two, HEAD_DIM), jnp.bfloat16)

    def wait_rest(slot):
        settle(bufs[slot].at[:, pl.ds(0, keys)], far_recv.at[slot])

        @pl.when(has_rim)
        def _():
            settle(bufs[slot].at[:, pl.ds(0, two)], rim_recv.at[slot])

    key_row = lax.broadcasted_iota(jnp.int32, (1, keys), 1) // cols
    distance = jnp.where(key_row == half, 0, 1)
    distance = jnp.where(jnp.logical_and(key_row == 2, no_rim), 9, distance)
    factor = HEAD_DIM ** -0.5 * 1.4426950408889634

    def spreads(frame):
        targets = [kf_ref[j, frame] for j in range(slots)]
        spans = [jnp.where(j < used_ref[frame], reach_ref[j, frame], -1) for j in range(slots)]
        found = []
        for j in range(slots):
            spread = spans[j]
            for i in range(slots):
                if i != j:
                    spread = jnp.maximum(spread, jnp.where(targets[i] == targets[j], spans[i], -1))
            for i in range(j):
                spread = jnp.where(jnp.logical_and(targets[i] == targets[j], spans[i] >= 0), -1, spread)
            found.append(jnp.where(spans[j] >= 0, spread, -1))
        return targets, found

    def seen(buf, frame, which):
        return jnp.concatenate([buf[frame, pl.ds((2 * i + which) * cols, cols), :] for i in range(3)], axis=0)

    def attend(group, slot):
        buf = bufs[slot]
        masks = [spreads(frame) for frame in group]
        scores = [
            [
                lax.dot_general(
                    buf[frame, pl.ds(q_at, cols), :], seen(buf, target, 0),
                    (((1,), (1,)), ((), ())), preferred_element_type=jnp.float32,
                )
                for target in targets
            ]
            for frame, (targets, _) in zip(group, masks)
        ]
        weights, totals = [], []
        for row, (_, found) in zip(scores, masks):
            row = [s * factor + jnp.where(distance <= spread, 0.0, NEG) for s, spread in zip(row, found)]
            peak = jnp.max(functools.reduce(jnp.maximum, row), axis=1, keepdims=True)
            row = [jnp.exp2(s - peak) for s in row]
            totals.append(jnp.sum(functools.reduce(jnp.add, row), axis=1, keepdims=True))
            weights.append(row)
        mixed = [
            functools.reduce(jnp.add, [
                lax.dot_general(
                    w.astype(jnp.bfloat16), seen(buf, target, 1),
                    (((1,), (0,)), ((), ())), preferred_element_type=jnp.float32,
                )
                for w, target in zip(row, targets)
            ])
            for row, (targets, _) in zip(weights, masks)
        ]
        for frame, value, total in zip(group, mixed, totals):
            outs[slot][frame] = (value / total).astype(jnp.bfloat16)

    out_col = [pl.multiple_of(head_of(me, slot) * HEAD_DIM, HEAD_DIM) for slot in range(2)]
    out_row = pl.multiple_of(half * cols, cols)

    def send_out(frame, slot):
        view = o_ref.at[pl.ds(out_row, cols), pl.ds(out_col[slot], HEAD_DIM)]

        @pl.when(frame == me)
        def _():
            pltpu.make_async_copy(outs[slot].at[frame], view, out_recv.at[slot]).start()

        @pl.when(frame != me)
        def _():
            pltpu.make_async_remote_copy(
                src_ref=outs[slot].at[frame], dst_ref=view, send_sem=out_send.at[slot], recv_sem=out_recv.at[slot],
                device_id=(frame, pair), device_id_type=MESH,
            ).start()

    def group_of(step, size):
        group = []
        for u in range(size // 2):
            t = size // 2 * step + u
            first = chip(6 - 4 * lax.rem(t, 2) - 2 * (lax.rem(t, 4) // 2) + t // 4, 1)
            group += [first, first + 1]
        return group

    @pl.when(no_rim)
    def _():
        clear_rim(0)
        clear_rim(1)

    @pl.loop(0, steps)
    def _(step):
        pass_rims(step, 0)
        send_far(step, 0)

    @pl.loop(0, steps)
    def _(step):
        send_far(step, 1)

        @pl.when(core == LARGE_CORE)
        def _():
            pass_rims(step, 1)

    for copy in mask_copies:
        copy.wait()

    wait_rest(0)

    @pl.loop(0, frames // GROUPS[0])
    def _(step):
        attend(group_of(step, GROUPS[0]), 0)

    @pl.loop(0, steps)
    def _(step):
        for frame in group_of(step, 2):
            send_out(frame, 0)

    @pl.when(core == LARGE_CORE)
    def _():
        wait_rest(1)

        @pl.loop(0, frames // GROUPS[1])
        def _(step):
            group = group_of(step, GROUPS[1])
            attend(group, 1)
            for frame in group:
                send_out(frame, 1)

    settle(buf_a.at[pl.ds(0, frames - 1), pl.ds(0, 2 * two + cols)], main_send.at[0])
    settle(out_a.at[pl.ds(0, frames - 1)], out_send.at[0])

    @pl.when(has_rim)
    def _():
        settle(buf_a.at[:, pl.ds(0, two)], rim_send.at[0])

    @pl.when(core == LARGE_CORE)
    def _():
        settle(buf_b.at[pl.ds(0, frames // 2 - 1), pl.ds(0, 2 * two + cols)], main_send.at[1])
        settle(out_b.at[pl.ds(0, frames - 1)], out_send.at[1])

        @pl.when(has_rim)
        def _():
            settle(buf_b.at[:, pl.ds(0, two)], rim_send.at[1])

    @pl.when(core != LARGE_CORE)
    def _():
        settle(buf_b.at[pl.ds(0, frames // 2), pl.ds(0, 2 * two + cols)], main_send.at[1])

    settle(out_a, out_recv.at[0])
    settle(out_b.at[pl.ds(0, frames // 2)], out_recv.at[1])


def local(query, key, value, key_frames, reach, used):
    _, rows, cols, features = query.shape
    frames, pairs = lax.axis_size("frame"), lax.axis_size("row")
    slots = key_frames.shape[1]
    flat = (rows * cols, features)
    block = (frames, 7 * cols, HEAD_DIM)
    out_block = (frames, cols, HEAD_DIM)
    hbm = pl.BlockSpec(memory_space=pl.ANY)
    out = pl.pallas_call(
        functools.partial(body, frames, pairs, cols, slots),
        out_shape=jax.ShapeDtypeStruct(flat, jnp.bfloat16),
        in_specs=[hbm] * 6,
        out_specs=hbm,
        scratch_shapes=[
            pltpu.VMEM(block, jnp.bfloat16),
            pltpu.VMEM(block, jnp.bfloat16),
            pltpu.VMEM(out_block, jnp.bfloat16),
            pltpu.VMEM(out_block, jnp.bfloat16),
            pltpu.SemaphoreType.DMA((2, frames)),
        ] + [pltpu.SemaphoreType.DMA((2,))] * 6 + [
            pltpu.SMEM((slots, frames), jnp.int32),
            pltpu.SMEM((slots, frames), jnp.int32),
            pltpu.SMEM((frames,), jnp.int32),
            pltpu.SemaphoreType.DMA((3,)),
        ],
        compiler_params=pltpu.CompilerParams(
            collective_id=0, has_side_effects=True, vmem_limit_bytes=53 * 1024 * 1024
        ),
        cost_estimate=pl.CostEstimate(flops=2 * 10**9, bytes_accessed=10**7, transcendentals=10**7),
    )(key_frames.T, reach.T, used, query.reshape(flat), key.reshape(flat), value.reshape(flat))
    return out.reshape(query.shape)


def solution(mesh):
    return jax.shard_map(
        local,
        mesh=mesh,
        in_specs=(
            P("frame", "row", None, None),
            P("frame", "row", None, None),
            P("frame", "row", None, None),
            P(),
            P(),
            P(),
        ),
        out_specs=P("frame", "row", None, None),
        check_vma=False,
    )
```

```python
import functools

import jax
import jax.numpy as jnp
from jax import lax
from jax.experimental import pallas as pl
from jax.experimental.pallas import tpu as pltpu
from jax.sharding import PartitionSpec as P


HEAD_DIM = 128
MESH = pl.DeviceIdType.MESH
NEG = -1e30
LARGE_CORE = 1
GROUPS = (8, 4)


def body(frames, pairs, cols, slots, kf_hbm, reach_hbm, used_hbm, q_ref, k_ref, v_ref, o_ref,
         buf_a, buf_b, out_a, out_b, near_recv, far_recv, main_send, rim_send, rim_recv, out_send, out_recv, kf_ref, reach_ref, used_ref, mask_sem, ready):
    me = lax.axis_index("frame")
    pair = lax.axis_index("row")
    core = lax.rem(me, 2)
    half = lax.rem(me // 2, 2)
    bufs, outs = (buf_a, buf_b), (out_a, out_b)
    keys = 3 * cols
    two = 2 * cols
    q_at = 2 * keys
    has_rim = jnp.logical_or(
        jnp.logical_and(half == 1, pair < pairs - 1), jnp.logical_and(half == 0, pair > 0)
    )
    no_rim = jnp.logical_not(has_rim)
    rim_pair = jnp.where(half == 1, pair + 1, pair - 1)
    rim_frame = 4 * (me // 4) + 2 * (1 - half) + core
    rim_row = pl.multiple_of(half * two, two)

    def head_of(device, slot):
        return 3 * (device // 4) + (2 * lax.rem(device + LARGE_CORE, 2) if slot == 0 else 1)

    def chip(step, sign):
        k = step // 2
        distance = k + k // 2 - 2 * (k // 2) * lax.rem(k, 2)
        x = lax.rem(me // 4 + 4 + sign * distance, 4)
        return 4 * x + 2 * lax.rem(half + 1 + step, 2)

    mask_copies = [
        pltpu.make_async_copy(src, dst, mask_sem.at[i])
        for i, (src, dst) in enumerate(((kf_hbm, kf_ref), (reach_hbm, reach_ref), (used_hbm, used_ref)))
    ]
    for copy in mask_copies:
        copy.start()

    barrier = pltpu.get_barrier_semaphore()

    across = me + 2 - 4 * half

    def greet(device):
        pl.semaphore_signal(barrier, inc=1, device_id=(device, pair), device_id_type=MESH)

    @pl.loop(1, frames // 2)
    def _(d):
        x = lax.rem(me // 4 + d // 2, 4)
        greet(4 * x + 2 * half + lax.rem(core + d, 2))

    greet(across)
    greet(across + 1 - 2 * core)

    @pl.when(has_rim)
    def _():
        pl.semaphore_signal(barrier, inc=1, device_id=(rim_frame, rim_pair), device_id_type=MESH)

    def piece(ref, device, slot, row, at):
        lanes = pl.ds(pl.multiple_of(head_of(device, slot) * HEAD_DIM, HEAD_DIM), HEAD_DIM)
        return (
            ref.at[pl.ds(pl.multiple_of(row * cols, cols), cols), lanes],
            bufs[slot].at[me, pl.ds(pl.multiple_of(at * cols, cols), cols)],
        )

    def half_of(device):
        return lax.rem(device // 2, 2)

    def near(device, slot):
        row = half_of(device)
        return piece(k_ref, device, slot, row, 2 * row), piece(v_ref, device, slot, row, 2 * row + 1)

    def far(device, slot):
        row = 1 - half_of(device)
        return (
            piece(k_ref, device, slot, row, 2 * row),
            piece(v_ref, device, slot, row, 2 * row + 1),
            piece(q_ref, device, slot, 1 - row, 6),
        )

    def keep(slot):
        for src, dst in near(me, slot):
            pltpu.make_async_copy(src, dst, near_recv.at[slot, me]).start()
        for src, dst in far(me, slot):
            pltpu.make_async_copy(src, dst, far_recv.at[slot]).start()

    def send(pieces, slot, recv_sem, device):
        for src, dst in pieces:
            pltpu.make_async_remote_copy(
                src_ref=src, dst_ref=dst, send_sem=main_send.at[slot], recv_sem=recv_sem,
                device_id=(device, pair), device_id_type=MESH,
            ).start()

    def settle(view, sem):
        pltpu.make_async_copy(view, view, sem).wait()

    keep(0)

    @pl.when(core == LARGE_CORE)
    def _():
        keep(1)

    @pl.when(has_rim)
    def _():
        pl.semaphore_wait(barrier, frames // 2 + 2)

    @pl.when(no_rim)
    def _():
        pl.semaphore_wait(barrier, frames // 2 + 1)

    pl.semaphore_signal(ready, inc=1, device_id=(across, pair), device_id_type=MESH)

    steps = frames // 2

    def send_near(step, slot):
        for c in range(2 - slot):
            device = chip(step, 1) + (c + LARGE_CORE) % 2

            @pl.when(device != me)
            def _():
                send(near(device, slot), slot, near_recv.at[slot, me], device)

    def send_far(step, slot):
        for c in range(2 - slot):
            device = chip(step, 1) + (c + LARGE_CORE) % 2

            @pl.when(device != me)
            def _():
                send(far(device, slot), slot, far_recv.at[slot], device)

    def early(i):
        return jnp.where(i == 7, 6, jnp.where(i == 6, 7, jnp.where(i == 5, 4, jnp.where(i == 4, 5, jnp.where(i == 3, 2, jnp.where(i == 2, 3, i))))))

    @pl.loop(0, 3)
    def _(i):
        send_near(early(i), 0)

    pl.semaphore_wait(ready, 1)

    @pl.loop(3, steps)
    def _(i):
        send_near(early(i), 0)

    @pl.loop(0, steps)
    def _(step):
        send_near(step, 1)

    def pass_rim(frame, slot):
        buf = bufs[slot]
        settle(buf.at[frame, pl.ds(0, two)], near_recv.at[slot, frame])

        @pl.when(has_rim)
        def _():
            pltpu.make_async_remote_copy(
                src_ref=buf.at[frame, pl.ds(rim_row, two)], dst_ref=buf.at[frame, pl.ds(2 * two, two)],
                send_sem=rim_send.at[slot], recv_sem=rim_recv.at[slot],
                device_id=(rim_frame, rim_pair), device_id_type=MESH,
            ).start()

    def pass_rims(step, slot):
        for c in range(2):
            pass_rim(chip(step, -1) + c, slot)

    def clear_rim(slot):
        @pl.loop(0, frames)
        def _(frame):
            bufs[slot][frame, pl.ds(2 * two, two), :] = jnp.zeros((two, HEAD_DIM), jnp.bfloat16)

    def wait_rest(slot):
        settle(bufs[slot].at[:, pl.ds(0, keys)], far_recv.at[slot])

        @pl.when(has_rim)
        def _():
            settle(bufs[slot].at[:, pl.ds(0, two)], rim_recv.at[slot])

    key_row = lax.broadcasted_iota(jnp.int32, (1, keys), 1) // cols
    distance = jnp.where(key_row == half, 0, 1)
    distance = jnp.where(jnp.logical_and(key_row == 2, no_rim), 9, distance)
    factor = HEAD_DIM ** -0.5 * 1.4426950408889634

    def spreads(frame):
        targets = [kf_ref[j, frame] for j in range(slots)]
        spans = [jnp.where(j < used_ref[frame], reach_ref[j, frame], -1) for j in range(slots)]
        found = []
        for j in range(slots):
            spread = spans[j]
            for i in range(slots):
                if i != j:
                    spread = jnp.maximum(spread, jnp.where(targets[i] == targets[j], spans[i], -1))
            for i in range(j):
                spread = jnp.where(jnp.logical_and(targets[i] == targets[j], spans[i] >= 0), -1, spread)
            found.append(jnp.where(spans[j] >= 0, spread, -1))
        return targets, found

    def seen(buf, frame, which):
        return jnp.concatenate([buf[frame, pl.ds((2 * i + which) * cols, cols), :] for i in range(3)], axis=0)

    def attend(group, slot):
        buf = bufs[slot]
        masks = [spreads(frame) for frame in group]
        scores = [
            [
                lax.dot_general(
                    buf[frame, pl.ds(q_at, cols), :], seen(buf, target, 0),
                    (((1,), (1,)), ((), ())), preferred_element_type=jnp.float32,
                )
                for target in targets
            ]
            for frame, (targets, _) in zip(group, masks)
        ]
        weights, totals = [], []
        for row, (_, found) in zip(scores, masks):
            row = [s * factor + jnp.where(distance <= spread, 0.0, NEG) for s, spread in zip(row, found)]
            peak = jnp.max(functools.reduce(jnp.maximum, row), axis=1, keepdims=True)
            row = [jnp.exp2(s - peak) for s in row]
            totals.append(jnp.sum(functools.reduce(jnp.add, row), axis=1, keepdims=True))
            weights.append(row)
        mixed = [
            functools.reduce(jnp.add, [
                lax.dot_general(
                    w.astype(jnp.bfloat16), seen(buf, target, 1),
                    (((1,), (0,)), ((), ())), preferred_element_type=jnp.float32,
                )
                for w, target in zip(row, targets)
            ])
            for row, (targets, _) in zip(weights, masks)
        ]
        for frame, value, total in zip(group, mixed, totals):
            outs[slot][frame] = (value / total).astype(jnp.bfloat16)

    out_col = [pl.multiple_of(head_of(me, slot) * HEAD_DIM, HEAD_DIM) for slot in range(2)]
    out_row = pl.multiple_of(half * cols, cols)

    def send_out(frame, slot):
        view = o_ref.at[pl.ds(out_row, cols), pl.ds(out_col[slot], HEAD_DIM)]

        @pl.when(frame == me)
        def _():
            pltpu.make_async_copy(outs[slot].at[frame], view, out_recv.at[slot]).start()

        @pl.when(frame != me)
        def _():
            pltpu.make_async_remote_copy(
                src_ref=outs[slot].at[frame], dst_ref=view, send_sem=out_send.at[slot], recv_sem=out_recv.at[slot],
                device_id=(frame, pair), device_id_type=MESH,
            ).start()

    def group_of(step, size):
        group = []
        for u in range(size // 2):
            t = size // 2 * step + u
            first = chip(6 - 4 * lax.rem(t, 2) - 2 * (lax.rem(t, 4) // 2) + t // 4, 1)
            group += [first, first + 1]
        return group

    @pl.when(no_rim)
    def _():
        clear_rim(0)
        clear_rim(1)

    @pl.loop(0, steps)
    def _(step):
        pass_rims(early(step), 0)
        send_far(step, 0)

    @pl.loop(0, steps)
    def _(step):
        send_far(step, 1)

        @pl.when(core == LARGE_CORE)
        def _():
            pass_rims(step, 1)

    for copy in mask_copies:
        copy.wait()

    wait_rest(0)

    @pl.loop(0, frames // GROUPS[0])
    def _(step):
        attend(group_of(step, GROUPS[0]), 0)

    @pl.loop(0, steps)
    def _(step):
        for frame in group_of(step, 2):
            send_out(frame, 0)

    @pl.when(core == LARGE_CORE)
    def _():
        wait_rest(1)

        @pl.loop(0, frames // GROUPS[1])
        def _(step):
            group = group_of(step, GROUPS[1])
            attend(group, 1)
            for frame in group:
                send_out(frame, 1)

    settle(buf_a.at[pl.ds(0, frames - 1), pl.ds(0, 2 * two + cols)], main_send.at[0])
    settle(out_a.at[pl.ds(0, frames - 1)], out_send.at[0])

    @pl.when(has_rim)
    def _():
        settle(buf_a.at[:, pl.ds(0, two)], rim_send.at[0])

    @pl.when(core == LARGE_CORE)
    def _():
        settle(buf_b.at[pl.ds(0, frames // 2 - 1), pl.ds(0, 2 * two + cols)], main_send.at[1])
        settle(out_b.at[pl.ds(0, frames - 1)], out_send.at[1])

        @pl.when(has_rim)
        def _():
            settle(buf_b.at[:, pl.ds(0, two)], rim_send.at[1])

    @pl.when(core != LARGE_CORE)
    def _():
        settle(buf_b.at[pl.ds(0, frames // 2), pl.ds(0, 2 * two + cols)], main_send.at[1])

    settle(out_a, out_recv.at[0])
    settle(out_b.at[pl.ds(0, frames // 2)], out_recv.at[1])


def local(query, key, value, key_frames, reach, used):
    _, rows, cols, features = query.shape
    frames, pairs = lax.axis_size("frame"), lax.axis_size("row")
    slots = key_frames.shape[1]
    flat = (rows * cols, features)
    block = (frames, 7 * cols, HEAD_DIM)
    out_block = (frames, cols, HEAD_DIM)
    hbm = pl.BlockSpec(memory_space=pl.ANY)
    out = pl.pallas_call(
        functools.partial(body, frames, pairs, cols, slots),
        out_shape=jax.ShapeDtypeStruct(flat, jnp.bfloat16),
        in_specs=[hbm] * 6,
        out_specs=hbm,
        scratch_shapes=[
            pltpu.VMEM(block, jnp.bfloat16),
            pltpu.VMEM(block, jnp.bfloat16),
            pltpu.VMEM(out_block, jnp.bfloat16),
            pltpu.VMEM(out_block, jnp.bfloat16),
            pltpu.SemaphoreType.DMA((2, frames)),
        ] + [pltpu.SemaphoreType.DMA((2,))] * 6 + [
            pltpu.SMEM((slots, frames), jnp.int32),
            pltpu.SMEM((slots, frames), jnp.int32),
            pltpu.SMEM((frames,), jnp.int32),
            pltpu.SemaphoreType.DMA((3,)),
            pltpu.SemaphoreType.REGULAR,
        ],
        compiler_params=pltpu.CompilerParams(
            collective_id=0, has_side_effects=True, vmem_limit_bytes=53 * 1024 * 1024
        ),
        cost_estimate=pl.CostEstimate(flops=2 * 10**9, bytes_accessed=10**7, transcendentals=10**7),
    )(key_frames.T, reach.T, used, query.reshape(flat), key.reshape(flat), value.reshape(flat))
    return out.reshape(query.shape)


def solution(mesh):
    return jax.shard_map(
        local,
        mesh=mesh,
        in_specs=(
            P("frame", "row", None, None),
            P("frame", "row", None, None),
            P("frame", "row", None, None),
            P(),
            P(),
            P(),
        ),
        out_specs=P("frame", "row", None, None),
        check_vma=False,
    )
```
